128 devices in a mesh: expert: 2 (over y_hi), fsdp: 64 (over x, y_lo, z, core).
Axes of the slice: x: 4, y: 4 (y_hi: 2, y_lo: 2; y = y_hi * 2 + y_lo), z: 4, core: 2. Of those that a mesh axis runs over, the one named last changes fastest.
Arguments:
- query_rows: bfloat16 [32768, 2560], P(('expert', 'fsdp')), may hold values from -16 to 16
- key_rows: bfloat16 [32768, 2560], P(('expert', 'fsdp')), may hold values from -16 to 16
- value_rows: bfloat16 [32768, 2560], P(('expert', 'fsdp')), may hold values from -6 to 6
- timestep: int32 [32], replicated, may hold values from 0 to 999, as said below
- time_weight: bfloat16 [2, 256, 5120], P('expert', None, 'fsdp'), may hold values from -0.375 to 0.375
- gate_weight: bfloat16 [2, 5120, 2560], P('expert', None, 'fsdp'), may hold values from -0.078125 to 0.078125
- cotangent: bfloat16 [32768, 2560], P(('expert', 'fsdp')), may hold values from -6 to 6
Outputs:
- gated: bfloat16 [32768, 2560], P(('expert', 'fsdp'))
- query_grad: bfloat16 [32768, 2560], P(('expert', 'fsdp'))
- key_grad: bfloat16 [32768, 2560], P(('expert', 'fsdp'))
- value_grad: bfloat16 [32768, 2560], P(('expert', 'fsdp'))
- time_grad: float32 [2, 256, 5120], P('expert', None, 'fsdp')
- gate_grad: float32 [2, 5120, 2560], P('expert', None, 'fsdp')
The draws below stay inside these ranges and needn't reach their ends.
Inputs may be any that keep to these rules, and one draw needn't show every extreme that they name: Exactly half of the clips have a timestep of 875 or more.
All inputs are finite; a program needn't handle non-finite values.
Results may differ from the reference program's by a relative error of at most 0.03.
Values may be sent and summed in bfloat16 or wider, within the bound.
A program may use at most 192 MiB of HBM per device.

```python
import math
import jax
import jax.numpy as jnp
from jax import lax

D = 5120
FREQ = 256
HEAD = 128
HEADS = 20
BOUNDARY = 875
SPAN = 4
ROWS = 256
DH = 2560
CLIP = 1024
NCLIP = 32
TOKENS = 32768
N_FSDP = 64


def draw_query_rows(key, part):
    key = jax.random.fold_in(key, 1)
    own_rows = jax.random.normal(key, (TOKENS, DH), jnp.float32)
    return jnp.clip(own_rows, -16.0, 16.0).astype(jnp.bfloat16)


def draw_key_rows(key, part):
    key = jax.random.fold_in(key, 2)
    own_rows = jax.random.normal(key, (TOKENS, DH), jnp.float32)
    return jnp.clip(own_rows, -16.0, 16.0).astype(jnp.bfloat16)


def draw_timestep(key, part):
    key = jax.random.fold_in(key, 7)
    order = jax.random.permutation(jax.random.fold_in(key, 1), NCLIP)
    high_steps = jax.random.randint(jax.random.fold_in(key, 2), (NCLIP,), BOUNDARY, 1000)
    low_steps = jax.random.randint(jax.random.fold_in(key, 3), (NCLIP,), 0, BOUNDARY)
    return jnp.where(order < NCLIP // 2, high_steps, low_steps).astype(jnp.int32)


def block_levels(stream_key, shape, pieces, smallest, largest):
    level, own = 1.0, jax.random.fold_in(stream_key, 6)
    for dim, blocks in pieces:
        steps = jnp.exp(jax.random.uniform(jax.random.fold_in(own, dim), (blocks,), jnp.float32, smallest / len(pieces), largest / len(pieces)))
        level = level * jnp.repeat(steps, shape[dim] // blocks).reshape([-1 if axis == dim else 1 for axis in range(len(shape))])
    return level


def normal_values(stream_key, extent, deviation, limit, shards=(), held_as=jnp.bfloat16):
    result = deviation * jax.random.normal(stream_key, extent, jnp.float32)
    if shards:
        result = result * block_levels(stream_key, extent, shards, -0.22, 0.18)
    return jnp.clip(result, -limit, limit).astype(held_as)


def setup_inputs(seed: int = 0) -> dict:
    key_of = jax.random.split(jax.random.key(seed), 8)
    return {
        "query_rows": draw_query_rows(jax.random.fold_in(key_of[7], 71), 0),
        "key_rows": draw_key_rows(jax.random.fold_in(key_of[7], 71), 0),
        "value_rows": normal_values(key_of[2], (TOKENS, DH), 1.0, 6.0, ((0, 128),)),
        "timestep": draw_timestep(jax.random.fold_in(key_of[7], 71), 0),
        "time_weight": normal_values(key_of[4], (2, FREQ, D), FREQ ** -0.5, 0.375, ((0, 2), (2, 64))),
        "gate_weight": normal_values(key_of[5], (2, D, DH), D ** -0.5, 0.078125, ((0, 2), (2, 64))),
        "cotangent": normal_values(key_of[6], (TOKENS, DH), 1.0, 6.0, ((0, 128),)),
    }


def sinusoid(timestep):
    half_freq = FREQ // 2
    indices = jnp.arange(half_freq, dtype=jnp.float32)
    frequency = jnp.exp(-math.log(10000.0) * indices / half_freq)
    angles = timestep.astype(jnp.float32)[:, None] * frequency[None, :]
    return jnp.concatenate([jnp.cos(angles), jnp.sin(angles)], axis=1)


def to_clips(rows):
    stride = N_FSDP // SPAN
    return rows.reshape(2, SPAN, stride, ROWS, DH).transpose(0, 2, 1, 3, 4).reshape(NCLIP, CLIP, DH)


def from_clips(clips):
    stride = N_FSDP // SPAN
    return clips.reshape(2, stride, SPAN, ROWS, DH).transpose(0, 2, 1, 3, 4).reshape(TOKENS, DH)


def one_clip(inputs):
    query, keyed, valued, gate_row, cotan = inputs
    scaling = HEAD ** -0.5
    queries = query.astype(jnp.float32).reshape(CLIP, HEADS, HEAD)
    keys_f = keyed.astype(jnp.float32).reshape(CLIP, HEADS, HEAD)
    values_f = valued.astype(jnp.float32).reshape(CLIP, HEADS, HEAD)
    scores = jnp.einsum("qhd,khd->hqk", queries, keys_f) * scaling
    top = jnp.max(scores, axis=2, keepdims=True)
    expo = jnp.exp(scores - top)
    probability = expo / jnp.sum(expo, axis=2, keepdims=True)
    prob_half = probability.astype(jnp.bfloat16).astype(jnp.float32)
    attended = jnp.einsum("hqk,khd->qhd", prob_half, values_f).reshape(CLIP, DH).astype(jnp.bfloat16)
    gate_f = gate_row.astype(jnp.float32)[None, :]
    gated = (gate_f * attended.astype(jnp.float32)).astype(jnp.bfloat16)
    d_attended = (cotan.astype(jnp.float32) * gate_f).astype(jnp.bfloat16)
    d_gate = jnp.sum(cotan.astype(jnp.float32) * attended.astype(jnp.float32), axis=0)
    d_heads = d_attended.astype(jnp.float32).reshape(CLIP, HEADS, HEAD)
    delta = jnp.sum(d_heads * attended.astype(jnp.float32).reshape(CLIP, HEADS, HEAD), axis=2).T
    d_prob = jnp.einsum("qhd,khd->hqk", d_heads, values_f)
    d_scores = (probability * (d_prob - delta[:, :, None]) * scaling).astype(jnp.bfloat16).astype(jnp.float32)
    query_grad = jnp.einsum("hqk,khd->qhd", d_scores, keys_f).reshape(CLIP, DH).astype(jnp.bfloat16)
    key_grad = jnp.einsum("hqk,qhd->khd", d_scores, queries).reshape(CLIP, DH).astype(jnp.bfloat16)
    value_grad = jnp.einsum("hqk,qhd->khd", prob_half, d_heads).reshape(CLIP, DH).astype(jnp.bfloat16)
    return gated, query_grad, key_grad, value_grad, d_gate


def reference(query_rows, key_rows, value_rows, timestep, time_weight, gate_weight, cotangent):
    highest = lax.Precision.HIGHEST
    expert_of = (timestep >= BOUNDARY).astype(jnp.int32)
    sinusoid_rows = sinusoid(timestep)
    embeddings = []
    activations = []
    gate_all = []
    for expert in range(2):
        embedding = jnp.dot(sinusoid_rows, time_weight[expert].astype(jnp.float32), precision=highest).astype(jnp.bfloat16)
        activated = jax.nn.silu(embedding.astype(jnp.float32)).astype(jnp.bfloat16)
        gate_e = jnp.dot(activated, gate_weight[expert], preferred_element_type=jnp.float32).astype(jnp.bfloat16)
        embeddings.append(embedding)
        activations.append(activated)
        gate_all.append(gate_e)
    gate_table = jnp.where((expert_of == 1)[:, None], gate_all[1], gate_all[0])
    outputs = lax.map(one_clip, (to_clips(query_rows), to_clips(key_rows), to_clips(value_rows), gate_table, to_clips(cotangent)))
    gated, query_grad, key_grad, value_grad, d_gate = outputs
    time_grads = []
    gate_grads = []
    for expert in range(2):
        masked = jnp.where((expert_of == expert)[:, None], d_gate, 0.0)
        gate_grads.append(jnp.dot(activations[expert].astype(jnp.float32).T, masked, precision=highest))
        d_act = jnp.dot(masked, gate_weight[expert].astype(jnp.float32).T, precision=highest)
        emb_f = embeddings[expert].astype(jnp.float32)
        sig = jax.nn.sigmoid(emb_f)
        d_emb = d_act * sig * (1.0 + emb_f * (1.0 - sig))
        time_grads.append(jnp.dot(sinusoid_rows.T, d_emb, precision=highest))
    return (from_clips(gated), from_clips(query_grad), from_clips(key_grad), from_clips(value_grad), jnp.stack(time_grads), jnp.stack(gate_grads))
```

```python
import math

import jax
import jax.numpy as jnp
from jax import lax
from jax.experimental import pallas as pl
from jax.experimental.pallas import tpu as pltpu
from jax.sharding import PartitionSpec as P

FREQ = 256
HEAD = 128
BOUNDARY = 875
SPAN = 4
ROWS = 256
OWN = 5
CLIP = SPAN * ROWS
NCLIP = 32
EMB = 80
COLS = 40
D = 5120
DH = 2560
GROUP = 8 * EMB
QB = 256
MESH = pl.DeviceIdType.MESH
F32 = jnp.float32
BF16 = jnp.bfloat16
NT = (((1,), (1,)), ((), ()))
NN = (((1,), (0,)), ((), ()))


def dot(a, b, dims=NN):
    return lax.dot_general(a, b, dims, preferred_element_type=F32)


def split3(value):
    high = value.astype(BF16)
    rest = value - high.astype(F32)
    middle = rest.astype(BF16)
    return high, middle, (rest - middle.astype(F32)).astype(BF16)


def exact_dot(a, b, dims=NN):
    parts = split3(a)
    return dot(parts[0], b, dims) + (dot(parts[1], b, dims) + dot(parts[2], b, dims))


def kernel(
    ts, q_in, k_in, v_in, c_in, tw, gw,
    gated, query_grad, key_grad, value_grad, time_grad, gate_grad,
    buf, ost, emb, own_emb, act, sins, cols, cols_in, table, gate_rows,
    dg_own, dg_all, parts, sum_core, sum_z, sum_y, in_core, in_z, in_y, in_x,
    key_t, value_t, key_acc, value_acc,
    send_sems, recv_sems, in_send, in_recv, out_send, out_recv,
):
    half = lax.axis_index("expert")
    fsdp = lax.axis_index("fsdp")
    core = lax.rem(fsdp, 2)
    z = lax.rem(lax.div(fsdp, 2), 4)
    y = lax.rem(lax.div(fsdp, 8), 2)
    x = lax.div(fsdp, 16)
    plane = lax.rem(fsdp, 16)

    def place(x_, y_, z_, core_):
        return {"fsdp": x_ * 16 + y_ * 8 + z_ * 2 + core_}

    x_at = [lax.rem(x + d, 4) for d in (1, 2, 3)]
    z_at = [lax.rem(z + d, 4) for d in (1, 2, 3)]
    x_peers = [place(p, y, z, core) for p in x_at]
    z_peers = [place(x, y, p, core) for p in z_at]
    y_peer = place(x, 1 - y, z, core)
    core_peer = place(x, y, z, 1 - core)
    half_peer = {"expert": 1 - half}
    peers = x_peers + z_peers + [y_peer, core_peer, half_peer]

    barrier = pltpu.get_barrier_semaphore()
    for peer in peers:
        pl.semaphore_signal(barrier, inc=1, device_id=peer, device_id_type=MESH)

    used = [0]

    def begin(moves):
        copies = []
        for source, target, peer in moves:
            slot = used[0]
            used[0] += 1
            copy = pltpu.make_async_remote_copy(
                src_ref=source,
                dst_ref=target,
                send_sem=send_sems.at[slot],
                recv_sem=recv_sems.at[slot],
                device_id=peer,
                device_id_type=MESH,
            )
            copy.start()
            copies.append(copy)
        return copies

    def exchange(moves):
        for copy in begin(moves):
            copy.wait()

    row = lax.broadcasted_iota(jnp.int32, (NCLIP, HEAD), 0)
    lane = lax.broadcasted_iota(jnp.int32, (8, HEAD), 1)
    step_rows = jnp.zeros((NCLIP, HEAD), jnp.int32)
    step_lanes = jnp.zeros((8, HEAD), jnp.int32)
    for clip in range(NCLIP):
        step_rows = jnp.where(row == clip, ts[clip], step_rows)
        step_lanes = jnp.where(lane == clip, ts[clip], step_lanes)
    own_rows = (step_rows >= BOUNDARY).astype(jnp.int32) == half
    own_lanes = (step_lanes >= BOUNDARY).astype(jnp.int32) == half

    index = lax.broadcasted_iota(jnp.int32, (NCLIP, HEAD), 1).astype(F32)
    frequency = jnp.exp(-math.log(10000.0) * index / (FREQ // 2))
    angles = step_rows.astype(F32) * frequency
    sins[:, 0:HEAD] = jnp.cos(angles)
    sins[:, HEAD:FREQ] = jnp.sin(angles)
    emb_cols = exact_dot(sins[...], tw[...], NT)
    own_emb[...] = jnp.zeros(own_emb.shape, F32)
    own_emb[:, 0:EMB] = emb_cols
    emb[x, y, z, core] = own_emb[...].astype(BF16)

    pl.semaphore_wait(barrier, len(peers))

    first = begin([(emb.at[x, y, z, core], emb.at[x, y, z, core], peer) for peer in x_peers])
    sources = (q_in, k_in, v_in, c_in)

    def send_head(head, carry):
        for which, source in enumerate(sources):
            for to, peer in zip(x_at, x_peers):
                pltpu.make_async_remote_copy(
                    src_ref=source.at[:, pl.ds(pl.multiple_of((to * OWN + head) * HEAD, HEAD), HEAD)],
                    dst_ref=buf.at[head, which, pl.ds(pl.multiple_of(x * ROWS, ROWS), ROWS), :],
                    send_sem=in_send,
                    recv_sem=in_recv.at[head],
                    device_id=peer,
                    device_id_type=MESH,
                ).start()
            pltpu.make_async_copy(
                source.at[:, pl.ds(pl.multiple_of((x * OWN + head) * HEAD, HEAD), HEAD)],
                buf.at[head, which, pl.ds(pl.multiple_of(x * ROWS, ROWS), ROWS), :],
                in_recv.at[head],
            ).start()
        return carry

    lax.fori_loop(0, OWN, send_head, 0)

    for copy in first:
        copy.wait()
    exchange([(emb.at[:, y, z, core], emb.at[:, y, z, core], y_peer)])
    exchange([(emb.at[:, :, z, core], emb.at[:, :, z, core], peer) for peer in z_peers])
    exchange([(emb.at[:, :, :, core], emb.at[:, :, :, core], core_peer)])

    def activate(group, carry):
        x_, y_ = lax.div(group, 2), lax.rem(group, 2)
        blocks = [emb[x_, y_, j // 2, j % 2].astype(F32)[:, 0:EMB] for j in range(8)]
        value = jnp.concatenate(blocks, axis=1)
        value = value / (1.0 + jnp.exp(-value))
        act[:, pl.ds(pl.multiple_of(group * GROUP, GROUP), GROUP)] = value.astype(BF16)
        return carry

    lax.fori_loop(0, 8, activate, 0)
    gate_cols = dot(gw[...], act[...], NT).astype(BF16).astype(F32)
    cols[...] = jnp.zeros(cols.shape, F32)
    cols[:, 0:NCLIP] = gate_cols
    exchange([(cols, cols_in, half_peer)])
    table[y, z, core] = jnp.where(own_lanes[0:1], cols[...], cols_in[...])
    exchange([(table.at[y, z, core], table.at[y, z, core], peer) for peer in z_peers])
    exchange([(table.at[y, :, core], table.at[y, :, core], y_peer)])
    exchange([(table.at[:, :, core], table.at[:, :, core], core_peer)])
    whole = table[...].reshape(OWN * HEAD, HEAD)
    for head in range(OWN):
        gate_rows[head] = whole[head * HEAD : (head + 1) * HEAD].T
    clip_index = half * 16 + plane

    scaling = HEAD ** (-0.5)
    dg_own[...] = jnp.zeros(dg_own.shape, F32)

    def attend(head):
        pltpu.make_async_copy(buf.at[head], buf.at[head], in_recv.at[head]).wait()
        keys = buf[head, 1]
        values = buf[head, 2]
        key_t[...] = keys.T
        value_t[...] = values.T
        gate = gate_rows[head, pl.ds(clip_index, 1), :]
        key_acc[...] = jnp.zeros(key_acc.shape, F32)
        value_acc[...] = jnp.zeros(value_acc.shape, F32)

        def block(step, d_gate):
            rows = pl.ds(pl.multiple_of(step * QB, QB), QB)
            queries = buf[head, 0, rows, :]
            scores = dot(buf[head, 1], queries, NT)
            top = jnp.max(scores, axis=0, keepdims=True)
            expo = jnp.exp2((scores - top) * (scaling * math.log2(math.e)))
            probability = expo * (1.0 / jnp.sum(expo, axis=0, keepdims=True))
            prob_half = probability.astype(BF16)
            attended = dot(value_t[...], prob_half).T.astype(BF16).astype(F32)
            cotangent = buf[head, 3, rows, :].astype(F32)
            ost[head, 0, rows, :] = (gate * attended).astype(BF16)
            d_attended = (cotangent * gate).astype(BF16)
            delta = jnp.sum((d_attended.astype(F32) * attended).T, axis=0, keepdims=True)
            d_prob = dot(buf[head, 2], d_attended, NT)
            d_scores = (probability * (d_prob - delta)).astype(BF16)
            key_acc[...] += dot(d_scores, queries)
            value_acc[...] += dot(prob_half, d_attended)
            d_query = dot(key_t[...], d_scores).T * scaling
            ost[head, 1, rows, :] = d_query.astype(BF16)
            return d_gate + jnp.sum(cotangent * attended, axis=0, keepdims=True)

        d_gate = lax.fori_loop(0, CLIP // QB, block, jnp.zeros((1, HEAD), F32))
        ost[head, 2] = (key_acc[...] * scaling).astype(BF16)
        ost[head, 3] = value_acc[...].astype(BF16)
        dg_own[pl.ds(head, 1), :] = d_gate

    targets = (gated, query_grad, key_grad, value_grad)

    def send_out(head):
        at = pl.ds(pl.multiple_of((x * OWN + head) * HEAD, HEAD), HEAD)
        for which, target in enumerate(targets):
            for to, peer in zip(x_at, x_peers):
                pltpu.make_async_remote_copy(
                    src_ref=ost.at[head, which, pl.ds(pl.multiple_of(to * ROWS, ROWS), ROWS), :],
                    dst_ref=target.at[:, at],
                    send_sem=out_send,
                    recv_sem=out_recv.at[which],
                    device_id=peer,
                    device_id_type=MESH,
                ).start()
            pltpu.make_async_copy(
                ost.at[head, which, pl.ds(pl.multiple_of(x * ROWS, ROWS), ROWS), :],
                target.at[:, at],
                out_recv.at[which],
            ).start()

    def run_head(head, carry):
        attend(head)
        send_out(head)
        return carry

    lax.fori_loop(0, OWN - 1, run_head, 0)
    attend(OWN - 1)

    dg_all[half, y, z, core] = dg_own[...]
    exchange([(dg_all.at[half, y, z, core], dg_all.at[half, y, z, core], peer) for peer in z_peers])
    exchange([(dg_all.at[half, y, :, core], dg_all.at[half, y, :, core], y_peer)])
    exchange([(dg_all.at[half, :, :, core], dg_all.at[half, :, :, core], core_peer)])
    exchange([(dg_all.at[half], dg_all.at[half], half_peer)])
    everything = dg_all[...].reshape(NCLIP, 8, HEAD)
    d_rows = jnp.zeros((NCLIP, COLS), F32)
    d_cols = jnp.zeros((COLS, NCLIP), F32)
    pick_row = lax.broadcasted_iota(jnp.int32, (COLS, HEAD), 0) + plane * COLS
    pick_lane = lax.broadcasted_iota(jnp.int32, (COLS, HEAD), 1)
    for head in range(OWN):
        pick = (pick_row == pick_lane + head * HEAD).astype(F32).astype(BF16)
        for part in split3(everything[:, head, :]):
            d_rows = d_rows + dot(part, pick, NT)
            d_cols = d_cols + dot(pick, part, NT)
    d_rows = jnp.where(own_rows[:, 0:COLS], d_rows, 0.0)
    d_cols = jnp.where(own_lanes[0:1, 0:NCLIP], d_cols, 0.0)
    row_parts = split3(d_rows)
    col_parts = split3(d_cols)
    parts[...] = jnp.zeros(parts.shape, F32)

    def weight_group(group, carry):
        at = pl.ds(pl.multiple_of(group * GROUP, GROUP), GROUP)
        weights = gw[:, at]
        value = dot(row_parts[0], weights) + (dot(row_parts[1], weights) + dot(row_parts[2], weights))
        for j in range(8):
            parts[lax.div(group, 2), lax.rem(group, 2), j // 2, j % 2, :, 0:EMB] = value[
                :, j * EMB : (j + 1) * EMB
            ]
        return carry

    lax.fori_loop(0, 8, weight_group, 0)

    copies = begin([(parts.at[:, :, :, 1 - core], in_core, core_peer)])

    def grad_group(group, carry):
        at = pl.ds(pl.multiple_of(group * GROUP, GROUP), GROUP)
        a = act[:, at]
        gate_grad[:, at] = dot(col_parts[0], a) + (dot(col_parts[1], a) + dot(col_parts[2], a))
        return carry

    lax.fori_loop(0, 8, grad_group, 0)

    copies[0].wait()
    sum_core[...] = parts[:, :, :, core] + in_core[...]
    exchange([(sum_core.at[:, :, p], in_z.at[d], peer) for d, (p, peer) in enumerate(zip(z_at, z_peers))])
    sum_z[...] = sum_core[:, :, z] + ((in_z[0] + in_z[1]) + in_z[2])
    exchange([(sum_z.at[:, 1 - y], in_y, y_peer)])
    sum_y[...] = sum_z[:, y] + in_y[...]
    copies = begin([(sum_y.at[p], in_x.at[d], peer) for d, (p, peer) in enumerate(zip(x_at, x_peers))])
    send_out(OWN - 1)
    for copy in copies:
        copy.wait()
    d_act = sum_y[x] + ((in_x[0] + in_x[1]) + in_x[2])
    value = emb[x, y, z, core].astype(F32)
    sigmoid = 1.0 / (1.0 + jnp.exp(-value))
    d_emb = d_act * sigmoid * (1.0 + value * (1.0 - sigmoid))
    d_emb = jnp.concatenate([d_emb, jnp.zeros((HEAD - NCLIP, HEAD), F32)], axis=0).T
    result = lax.dot_general(
        d_emb[0:EMB, 0:NCLIP], sins[...], NN,
        precision=lax.Precision.HIGHEST, preferred_element_type=F32,
    )
    time_grad[...] = result

    sent = buf.at[:, :, pl.ds(0, CLIP - ROWS), :]
    pltpu.make_async_copy(sent, sent, in_send).wait()
    sent = ost.at[:, :, pl.ds(0, CLIP - ROWS), :]
    pltpu.make_async_copy(sent, sent, out_send).wait()
    for which, target in enumerate(targets):
        pltpu.make_async_copy(target, target, out_recv.at[which]).wait()


def per_device(query_rows, key_rows, value_rows, timestep, time_weight, gate_weight, cotangent):
    anywhere = pl.BlockSpec(memory_space=pl.ANY)
    vmem = pl.BlockSpec(memory_space=pltpu.VMEM)
    rows = jax.ShapeDtypeStruct((ROWS, DH), BF16)
    blocks = (SPAN, 2, 4, 2)
    outs = pl.pallas_call(
        kernel,
        out_shape=(
            rows, rows, rows, rows,
            jax.ShapeDtypeStruct((EMB, FREQ), F32),
            jax.ShapeDtypeStruct((COLS, D), F32),
        ),
        in_specs=[pl.BlockSpec(memory_space=pltpu.SMEM)] + [anywhere] * 4 + [vmem] * 2,
        out_specs=(anywhere,) * 4 + (vmem,) * 2,
        scratch_shapes=[
            pltpu.VMEM((OWN, 4, CLIP, HEAD), BF16),
            pltpu.VMEM((OWN, 4, CLIP, HEAD), BF16),
            pltpu.VMEM(blocks + (NCLIP, HEAD), BF16),
            pltpu.VMEM((NCLIP, HEAD), F32),
            pltpu.VMEM((NCLIP, D), BF16),
            pltpu.VMEM((NCLIP, FREQ), F32),
            pltpu.VMEM((COLS, HEAD), F32),
            pltpu.VMEM((COLS, HEAD), F32),
            pltpu.VMEM(blocks[1:] + (COLS, HEAD), F32),
            pltpu.VMEM((OWN, HEAD, HEAD), F32),
            pltpu.VMEM((8, HEAD), F32),
            pltpu.VMEM((2,) + blocks[1:] + (8, HEAD), F32),
            pltpu.VMEM(blocks + (NCLIP, HEAD), F32),
            pltpu.VMEM(blocks[:3] + (NCLIP, HEAD), F32),
            pltpu.VMEM(blocks[:2] + (NCLIP, HEAD), F32),
            pltpu.VMEM(blocks[:1] + (NCLIP, HEAD), F32),
            pltpu.VMEM(blocks[:3] + (NCLIP, HEAD), F32),
            pltpu.VMEM((3,) + blocks[:2] + (NCLIP, HEAD), F32),
            pltpu.VMEM(blocks[:1] + (NCLIP, HEAD), F32),
            pltpu.VMEM((3, NCLIP, HEAD), F32),
            pltpu.VMEM((HEAD, CLIP), BF16),
            pltpu.VMEM((HEAD, CLIP), BF16),
            pltpu.VMEM((CLIP, HEAD), F32),
            pltpu.VMEM((CLIP, HEAD), F32),
            pltpu.SemaphoreType.DMA((28,)),
            pltpu.SemaphoreType.DMA((28,)),
            pltpu.SemaphoreType.DMA,
            pltpu.SemaphoreType.DMA((OWN,)),
            pltpu.SemaphoreType.DMA,
            pltpu.SemaphoreType.DMA((4,)),
        ],
        compiler_params=pltpu.CompilerParams(
            collective_id=0, has_side_effects=True, vmem_limit_bytes=56 * 2**20
        ),
    )(
        timestep, query_rows, key_rows, value_rows, cotangent,
        time_weight[0].T, gate_weight[0].T,
    )
    gated, query_grad, key_grad, value_grad, time_grad, gate_grad = outs
    return gated, query_grad, key_grad, value_grad, time_grad.T[None], gate_grad.T[None]


def solution(mesh):
    return jax.shard_map(
        per_device,
        mesh=mesh,
        in_specs=(
            P(("expert", "fsdp"), None),
            P(("expert", "fsdp"), None),
            P(("expert", "fsdp"), None),
            P(),
            P("expert", None, "fsdp"),
            P("expert", None, "fsdp"),
            P(("expert", "fsdp"), None),
        ),
        out_specs=(
            P(("expert", "fsdp"), None),
            P(("expert", "fsdp"), None),
            P(("expert", "fsdp"), None),
            P(("expert", "fsdp"), None),
            P("expert", None, "fsdp"),
            P("expert", None, "fsdp"),
        ),
        check_vma=False,
    )
```

```python
import math

import jax
import jax.numpy as jnp
from jax import lax
from jax.experimental import pallas as pl
from jax.experimental.pallas import tpu as pltpu
from jax.sharding import PartitionSpec as P

FREQ = 256
HEAD = 128
BOUNDARY = 875
SPAN = 4
ROWS = 256
OWN = 5
CLIP = SPAN * ROWS
NCLIP = 32
EMB = 80
COLS = 40
D = 5120
DH = 2560
GROUP = 8 * EMB
QB = 256
MESH = pl.DeviceIdType.MESH
F32 = jnp.float32
BF16 = jnp.bfloat16
NT = (((1,), (1,)), ((), ()))
NN = (((1,), (0,)), ((), ()))


def dot(a, b, dims=NN):
    return lax.dot_general(a, b, dims, preferred_element_type=F32)


def split3(value):
    high = value.astype(BF16)
    rest = value - high.astype(F32)
    middle = rest.astype(BF16)
    return high, middle, (rest - middle.astype(F32)).astype(BF16)


def exact_dot(a, b, dims=NN):
    parts = split3(a)
    return dot(parts[0], b, dims) + (dot(parts[1], b, dims) + dot(parts[2], b, dims))


def kernel(
    ts_in, q_in, k_in, v_in, c_in, tw_in, gw_in,
    gated, query_grad, key_grad, value_grad, time_grad, gate_grad,
    ts, tw, gw, buf, ost, emb, own_emb, act, sins, cols, cols_in, table, gate_rows,
    dg_own, dg_all, parts, sum_core, sum_z, sum_y, in_core, in_z, in_y, in_x,
    key_t, value_t, key_acc, value_acc,
    ready, weight_sems, send_sems, recv_sems, in_send, in_recv, out_send, out_recv,
):
    half = lax.axis_index("expert")
    fsdp = lax.axis_index("fsdp")
    core = lax.rem(fsdp, 2)
    z = lax.rem(lax.div(fsdp, 2), 4)
    y = lax.rem(lax.div(fsdp, 8), 2)
    x = lax.div(fsdp, 16)
    plane = lax.rem(fsdp, 16)

    def place(x_, y_, z_, core_):
        return {"fsdp": x_ * 16 + y_ * 8 + z_ * 2 + core_}

    x_at = [lax.rem(x + d, 4) for d in (1, 2, 3)]
    z_at = [lax.rem(z + d, 4) for d in (1, 2, 3)]
    x_peers = [place(p, y, z, core) for p in x_at]
    z_peers = [place(x, y, p, core) for p in z_at]
    y_peer = place(x, 1 - y, z, core)
    core_peer = place(x, y, z, 1 - core)
    half_peer = {"expert": 1 - half}

    barrier = pltpu.get_barrier_semaphore()
    ahead = [z < p for p in z_at] + [y == 0, core == 1, half == 0]
    others = z_peers + [y_peer, core_peer, half_peer]
    for peer in x_peers:
        pl.semaphore_signal(barrier, inc=1, device_id=peer, device_id_type=MESH)
    for first, peer in zip(ahead, others):
        @pl.when(first)
        def _():
            pl.semaphore_signal(barrier, inc=1, device_id=peer, device_id_type=MESH)

    step_copy = pltpu.make_async_copy(ts_in, ts, weight_sems.at[2])
    step_copy.start()
    time_copy = pltpu.make_async_copy(tw_in, tw, weight_sems.at[0])
    time_copy.start()
    gate_copy = pltpu.make_async_copy(gw_in, gw, weight_sems.at[1])
    gate_copy.start()

    used = [0]

    def begin(moves):
        copies = []
        for source, target, peer in moves:
            slot = used[0]
            used[0] += 1
            copy = pltpu.make_async_remote_copy(
                src_ref=source,
                dst_ref=target,
                send_sem=send_sems.at[slot],
                recv_sem=recv_sems.at[slot],
                device_id=peer,
                device_id_type=MESH,
            )
            copy.start()
            copies.append(copy)
        return copies

    def exchange(moves):
        for copy in begin(moves):
            copy.wait()

    pl.semaphore_wait(barrier, 3 + z + y + (1 - core) + half)
    for first, peer in zip(ahead, others):
        @pl.when(jnp.logical_not(first))
        def _():
            pl.semaphore_signal(ready, inc=1, device_id=peer, device_id_type=MESH)

    sources = (q_in, k_in, v_in, c_in)

    def send_part(head, which):
        source = sources[which]
        target = buf.at[head, which, pl.ds(pl.multiple_of(x * ROWS, ROWS), ROWS), :]
        for to, peer in zip(x_at, x_peers):
            pltpu.make_async_remote_copy(
                src_ref=source.at[:, pl.ds(pl.multiple_of((to * OWN + head) * HEAD, HEAD), HEAD)],
                dst_ref=target,
                send_sem=in_send,
                recv_sem=in_recv.at[head],
                device_id=peer,
                device_id_type=MESH,
            ).start()
        pltpu.make_async_copy(
            source.at[:, pl.ds(pl.multiple_of((x * OWN + head) * HEAD, HEAD), HEAD)],
            target,
            in_recv.at[head],
        ).start()

    def send_head(head, carry):
        for which in range(4):
            send_part(head, which)
        return carry

    send_part(0, 0)

    row = lax.broadcasted_iota(jnp.int32, (NCLIP, HEAD), 0)
    lane = lax.broadcasted_iota(jnp.int32, (8, HEAD), 1)
    step_rows = jnp.zeros((NCLIP, HEAD), jnp.int32)
    step_lanes = jnp.zeros((8, HEAD), jnp.int32)
    step_copy.wait()
    for clip in range(NCLIP):
        step_rows = jnp.where(row == clip, ts[clip], step_rows)
        step_lanes = jnp.where(lane == clip, ts[clip], step_lanes)
    own_rows = (step_rows >= BOUNDARY).astype(jnp.int32) == half
    own_lanes = (step_lanes >= BOUNDARY).astype(jnp.int32) == half

    index = lax.broadcasted_iota(jnp.int32, (NCLIP, HEAD), 1).astype(F32)
    frequency = jnp.exp(-math.log(10000.0) * index / (FREQ // 2))
    angles = step_rows.astype(F32) * frequency
    sins[:, 0:HEAD] = jnp.cos(angles)
    sins[:, HEAD:FREQ] = jnp.sin(angles)
    time_copy.wait()
    emb_cols = exact_dot(sins[...], tw[...], NT)
    own_emb[...] = jnp.zeros(own_emb.shape, F32)
    own_emb[:, 0:EMB] = emb_cols
    emb[x, y, z, core] = own_emb[...].astype(BF16)
    first = begin([(emb.at[x, y, z, core], emb.at[x, y, z, core], peer) for peer in x_peers])
    for which in range(1, 4):
        send_part(0, which)
    lax.fori_loop(1, OWN, send_head, 0)

    for copy in first:
        copy.wait()
    later = (3 - z) + (1 - y) + core + (1 - half)

    @pl.when(later > 0)
    def _():
        pl.semaphore_wait(ready, later)

    exchange([(emb.at[:, y, z, core], emb.at[:, y, z, core], y_peer)])
    exchange([(emb.at[:, :, z, core], emb.at[:, :, z, core], peer) for peer in z_peers])
    exchange([(emb.at[:, :, :, core], emb.at[:, :, :, core], core_peer)])

    def activate(group, carry):
        x_, y_ = lax.div(group, 2), lax.rem(group, 2)
        blocks = [emb[x_, y_, j // 2, j % 2].astype(F32)[:, 0:EMB] for j in range(8)]
        value = jnp.concatenate(blocks, axis=1)
        value = value / (1.0 + jnp.exp(-value))
        act[:, pl.ds(pl.multiple_of(group * GROUP, GROUP), GROUP)] = value.astype(BF16)
        return carry

    lax.fori_loop(0, 8, activate, 0)
    gate_copy.wait()
    gate_cols = dot(gw[...], act[...], NT).astype(BF16).astype(F32)
    cols[...] = jnp.zeros(cols.shape, F32)
    cols[:, 0:NCLIP] = gate_cols
    exchange([(cols, cols_in, half_peer)])
    table[y, z, core] = jnp.where(own_lanes[0:1], cols[...], cols_in[...])
    exchange([(table.at[y, z, core], table.at[y, z, core], peer) for peer in z_peers])
    exchange([(table.at[y, :, core], table.at[y, :, core], y_peer)])
    exchange([(table.at[:, :, core], table.at[:, :, core], core_peer)])
    whole = table[...].reshape(OWN * HEAD, HEAD)
    for head in range(OWN):
        gate_rows[head] = whole[head * HEAD : (head + 1) * HEAD].T
    clip_index = half * 16 + plane

    scaling = HEAD ** (-0.5)
    dg_own[...] = jnp.zeros(dg_own.shape, F32)

    def attend(head):
        pltpu.make_async_copy(buf.at[head], buf.at[head], in_recv.at[head]).wait()
        keys = buf[head, 1]
        values = buf[head, 2]
        key_t[...] = keys.T
        value_t[...] = values.T
        gate = gate_rows[head, pl.ds(clip_index, 1), :]
        key_acc[...] = jnp.zeros(key_acc.shape, F32)
        value_acc[...] = jnp.zeros(value_acc.shape, F32)

        def block(step, d_gate):
            rows = pl.ds(pl.multiple_of(step * QB, QB), QB)
            queries = buf[head, 0, rows, :]
            scores = dot(buf[head, 1], queries, NT)
            top = jnp.max(scores, axis=0, keepdims=True)
            expo = jnp.exp2((scores - top) * (scaling * math.log2(math.e)))
            probability = expo * (1.0 / jnp.sum(expo, axis=0, keepdims=True))
            prob_half = probability.astype(BF16)
            attended = dot(value_t[...], prob_half).T.astype(BF16).astype(F32)
            cotangent = buf[head, 3, rows, :].astype(F32)
            ost[head, 0, rows, :] = (gate * attended).astype(BF16)
            d_attended = (cotangent * gate).astype(BF16)
            delta = jnp.sum((d_attended.astype(F32) * attended).T, axis=0, keepdims=True)
            d_prob = dot(buf[head, 2], d_attended, NT)
            d_scores = (probability * (d_prob - delta)).astype(BF16)
            key_acc[...] += dot(d_scores, queries)
            value_acc[...] += dot(prob_half, d_attended)
            d_query = dot(key_t[...], d_scores).T * scaling
            ost[head, 1, rows, :] = d_query.astype(BF16)
            return d_gate + jnp.sum(cotangent * attended, axis=0, keepdims=True)

        d_gate = lax.fori_loop(0, CLIP // QB, block, jnp.zeros((1, HEAD), F32))
        ost[head, 2] = (key_acc[...] * scaling).astype(BF16)
        ost[head, 3] = value_acc[...].astype(BF16)
        dg_own[pl.ds(head, 1), :] = d_gate

    targets = (gated, query_grad, key_grad, value_grad)

    def send_out(head):
        at = pl.ds(pl.multiple_of((x * OWN + head) * HEAD, HEAD), HEAD)
        for which, target in enumerate(targets):
            for to, peer in zip(x_at, x_peers):
                pltpu.make_async_remote_copy(
                    src_ref=ost.at[head, which, pl.ds(pl.multiple_of(to * ROWS, ROWS), ROWS), :],
                    dst_ref=target.at[:, at],
                    send_sem=out_send,
                    recv_sem=out_recv.at[which],
                    device_id=peer,
                    device_id_type=MESH,
                ).start()
            pltpu.make_async_copy(
                ost.at[head, which, pl.ds(pl.multiple_of(x * ROWS, ROWS), ROWS), :],
                target.at[:, at],
                out_recv.at[which],
            ).start()

    def run_head(head, carry):
        attend(head)
        send_out(head)
        return carry

    lax.fori_loop(0, OWN - 1, run_head, 0)
    attend(OWN - 1)

    dg_all[half, y, z, core] = dg_own[...]
    exchange([(dg_all.at[half, y, z, core], dg_all.at[half, y, z, core], peer) for peer in z_peers])
    exchange([(dg_all.at[half, y, :, core], dg_all.at[half, y, :, core], y_peer)])
    exchange([(dg_all.at[half, :, :, core], dg_all.at[half, :, :, core], core_peer)])
    exchange([(dg_all.at[half], dg_all.at[half], half_peer)])
    everything = dg_all[...].reshape(NCLIP, 8, HEAD)
    d_rows = jnp.zeros((NCLIP, COLS), F32)
    d_cols = jnp.zeros((COLS, NCLIP), F32)
    pick_row = lax.broadcasted_iota(jnp.int32, (COLS, HEAD), 0) + plane * COLS
    pick_lane = lax.broadcasted_iota(jnp.int32, (COLS, HEAD), 1)
    for head in range(OWN):
        pick = (pick_row == pick_lane + head * HEAD).astype(F32).astype(BF16)
        for part in split3(everything[:, head, :]):
            d_rows = d_rows + dot(part, pick, NT)
            d_cols = d_cols + dot(pick, part, NT)
    d_rows = jnp.where(own_rows[:, 0:COLS], d_rows, 0.0)
    d_cols = jnp.where(own_lanes[0:1, 0:NCLIP], d_cols, 0.0)
    row_parts = split3(d_rows)
    col_parts = split3(d_cols)
    parts[...] = jnp.zeros(parts.shape, F32)

    def weight_group(group, carry):
        at = pl.ds(pl.multiple_of(group * GROUP, GROUP), GROUP)
        weights = gw[:, at]
        value = dot(row_parts[0], weights) + (dot(row_parts[1], weights) + dot(row_parts[2], weights))
        for j in range(8):
            parts[lax.div(group, 2), lax.rem(group, 2), j // 2, j % 2, :, 0:EMB] = value[
                :, j * EMB : (j + 1) * EMB
            ]
        return carry

    lax.fori_loop(0, 8, weight_group, 0)

    copies = begin([(parts.at[:, :, :, 1 - core], in_core, core_peer)])

    def grad_group(group, carry):
        at = pl.ds(pl.multiple_of(group * GROUP, GROUP), GROUP)
        a = act[:, at]
        gate_grad[:, at] = dot(col_parts[0], a) + (dot(col_parts[1], a) + dot(col_parts[2], a))
        return carry

    lax.fori_loop(0, 8, grad_group, 0)

    copies[0].wait()
    sum_core[...] = parts[:, :, :, core] + in_core[...]
    exchange([(sum_core.at[:, :, p], in_z.at[d], peer) for d, (p, peer) in enumerate(zip(z_at, z_peers))])
    sum_z[...] = sum_core[:, :, z] + ((in_z[0] + in_z[1]) + in_z[2])
    exchange([(sum_z.at[:, 1 - y], in_y, y_peer)])
    sum_y[...] = sum_z[:, y] + in_y[...]
    copies = begin([(sum_y.at[p], in_x.at[d], peer) for d, (p, peer) in enumerate(zip(x_at, x_peers))])
    send_out(OWN - 1)
    for copy in copies:
        copy.wait()
    d_act = sum_y[x] + ((in_x[0] + in_x[1]) + in_x[2])
    value = emb[x, y, z, core].astype(F32)
    sigmoid = 1.0 / (1.0 + jnp.exp(-value))
    d_emb = d_act * sigmoid * (1.0 + value * (1.0 - sigmoid))
    d_emb = jnp.concatenate([d_emb, jnp.zeros((HEAD - NCLIP, HEAD), F32)], axis=0).T
    result = lax.dot_general(
        d_emb[0:EMB, 0:NCLIP], sins[...], NN,
        precision=lax.Precision.HIGHEST, preferred_element_type=F32,
    )
    time_grad[...] = result

    sent = buf.at[:, :, pl.ds(0, CLIP - ROWS), :]
    pltpu.make_async_copy(sent, sent, in_send).wait()
    sent = ost.at[:, :, pl.ds(0, CLIP - ROWS), :]
    pltpu.make_async_copy(sent, sent, out_send).wait()
    for which, target in enumerate(targets):
        pltpu.make_async_copy(target, target, out_recv.at[which]).wait()


def deliver(*refs):
    count = len(refs) // 2
    sems = refs[-1]
    copies = [
        pltpu.make_async_copy(refs[i], refs[count + i], sems.at[i]) for i in range(count)
    ]
    for copy in copies:
        copy.start()
    for copy in copies:
        copy.wait()


def per_device(query_rows, key_rows, value_rows, timestep, time_weight, gate_weight, cotangent):
    hbm = pl.BlockSpec(memory_space=pltpu.HBM)
    vmem = pl.BlockSpec(memory_space=pltpu.VMEM)
    blocks = (SPAN, 2, 4, 2)
    shapes = [((ROWS, DH), BF16)] * 4 + [((EMB, FREQ), F32), ((COLS, D), F32)]
    outs = pl.pallas_call(
        kernel,
        out_shape=tuple(pltpu.VMEM(shape, dtype) for shape, dtype in shapes),
        in_specs=[hbm] * 7,
        out_specs=(vmem,) * 6,
        scratch_shapes=[
            pltpu.SMEM((NCLIP,), jnp.int32),
            pltpu.VMEM((EMB, FREQ), BF16),
            pltpu.VMEM((COLS, D), BF16),
            pltpu.VMEM((OWN, 4, CLIP, HEAD), BF16),
            pltpu.VMEM((OWN, 4, CLIP, HEAD), BF16),
            pltpu.VMEM(blocks + (NCLIP, HEAD), BF16),
            pltpu.VMEM((NCLIP, HEAD), F32),
            pltpu.VMEM((NCLIP, D), BF16),
            pltpu.VMEM((NCLIP, FREQ), F32),
            pltpu.VMEM((COLS, HEAD), F32),
            pltpu.VMEM((COLS, HEAD), F32),
            pltpu.VMEM(blocks[1:] + (COLS, HEAD), F32),
            pltpu.VMEM((OWN, HEAD, HEAD), F32),
            pltpu.VMEM((8, HEAD), F32),
            pltpu.VMEM((2,) + blocks[1:] + (8, HEAD), F32),
            pltpu.VMEM(blocks + (NCLIP, HEAD), F32),
            pltpu.VMEM(blocks[:3] + (NCLIP, HEAD), F32),
            pltpu.VMEM(blocks[:2] + (NCLIP, HEAD), F32),
            pltpu.VMEM(blocks[:1] + (NCLIP, HEAD), F32),
            pltpu.VMEM(blocks[:3] + (NCLIP, HEAD), F32),
            pltpu.VMEM((3,) + blocks[:2] + (NCLIP, HEAD), F32),
            pltpu.VMEM(blocks[:1] + (NCLIP, HEAD), F32),
            pltpu.VMEM((3, NCLIP, HEAD), F32),
            pltpu.VMEM((HEAD, CLIP), BF16),
            pltpu.VMEM((HEAD, CLIP), BF16),
            pltpu.VMEM((CLIP, HEAD), F32),
            pltpu.VMEM((CLIP, HEAD), F32),
            pltpu.SemaphoreType.REGULAR,
            pltpu.SemaphoreType.DMA((3,)),
            pltpu.SemaphoreType.DMA((28,)),
            pltpu.SemaphoreType.DMA((28,)),
            pltpu.SemaphoreType.DMA,
            pltpu.SemaphoreType.DMA((OWN,)),
            pltpu.SemaphoreType.DMA,
            pltpu.SemaphoreType.DMA((4,)),
        ],
        compiler_params=pltpu.CompilerParams(
            collective_id=0, has_side_effects=True, vmem_limit_bytes=40 * 2**20
        ),
    )(
        *[
            pltpu.with_memory_space_constraint(array, pltpu.HBM)
            for array in (
                timestep, query_rows, key_rows, value_rows, cotangent,
                time_weight[0].T, gate_weight[0].T,
            )
        ],
    )
    outs = [pltpu.with_memory_space_constraint(out, pltpu.VMEM) for out in outs]
    outs = pl.pallas_call(
        deliver,
        out_shape=tuple(jax.ShapeDtypeStruct(shape, dtype) for shape, dtype in shapes),
        in_specs=[vmem] * 6,
        out_specs=(hbm,) * 6,
        scratch_shapes=[pltpu.SemaphoreType.DMA((6,))],
        compiler_params=pltpu.CompilerParams(vmem_limit_bytes=4 * 2**20),
    )(*outs)
    gated, query_grad, key_grad, value_grad, time_grad, gate_grad = outs
    return gated, query_grad, key_grad, value_grad, time_grad.T[None], gate_grad.T[None]


def solution(mesh):
    return jax.shard_map(
        per_device,
        mesh=mesh,
        in_specs=(
            P(("expert", "fsdp"), None),
            P(("expert", "fsdp"), None),
            P(("expert", "fsdp"), None),
            P(),
            P("expert", None, "fsdp"),
            P("expert", None, "fsdp"),
            P(("expert", "fsdp"), None),
        ),
        out_specs=(
            P(("expert", "fsdp"), None),
            P(("expert", "fsdp"), None),
            P(("expert", "fsdp"), None),
            P(("expert", "fsdp"), None),
            P("expert", None, "fsdp"),
            P("expert", None, "fsdp"),
        ),
        check_vma=False,
    )
```

```python
import math

import jax
import jax.numpy as jnp
from jax import lax
from jax.experimental import pallas as pl
from jax.experimental.pallas import tpu as pltpu
from jax.sharding import PartitionSpec as P

FREQ = 256
HEAD = 128
BOUNDARY = 875
SPAN = 4
ROWS = 256
OWN = 5
CLIP = SPAN * ROWS
NCLIP = 32
NOWN = 16
EMB = 80
COLS = 40
D = 5120
DH = 2560
GROUP = 8 * EMB
QB = 256
MESH = pl.DeviceIdType.MESH
F32 = jnp.float32
BF16 = jnp.bfloat16
NT = (((1,), (1,)), ((), ()))
NN = (((1,), (0,)), ((), ()))


def dot(a, b, dims=NN):
    return lax.dot_general(a, b, dims, preferred_element_type=F32)


def split3(value):
    high = value.astype(BF16)
    rest = value - high.astype(F32)
    middle = rest.astype(BF16)
    return high, middle, (rest - middle.astype(F32)).astype(BF16)


def exact_dot(a, b, dims=NN):
    parts = split3(a)
    return dot(parts[0], b, dims) + (dot(parts[1], b, dims) + dot(parts[2], b, dims))


def kernel(
    ts_in, q_in, k_in, v_in, c_in, tw_in, gw_in,
    gated, query_grad, key_grad, value_grad, time_grad, gate_grad,
    ts, tw, gw, buf, ost, emb, own_emb, act, sins, cols, cols_in, table, gate_rows,
    dg_own, dg_all, parts, sum_core, sum_z, sum_y, in_core, in_z, in_y, in_x, half_sums, pick_clip,
    key_t, value_t, key_acc, value_acc,
    ready, weight_sems, send_sems, recv_sems, in_send, in_recv, out_send, out_recv,
):
    half = lax.axis_index("expert")
    fsdp = lax.axis_index("fsdp")
    core = lax.rem(fsdp, 2)
    z = lax.rem(lax.div(fsdp, 2), 4)
    y = lax.rem(lax.div(fsdp, 8), 2)
    x = lax.div(fsdp, 16)
    plane = lax.rem(fsdp, 16)

    def place(x_, y_, z_, core_):
        return {"fsdp": x_ * 16 + y_ * 8 + z_ * 2 + core_}

    x_at = [lax.rem(x + d, 4) for d in (1, 2, 3)]
    z_at = [lax.rem(z + d, 4) for d in (1, 2, 3)]
    x_peers = [place(p, y, z, core) for p in x_at]
    z_peers = [place(x, y, p, core) for p in z_at]
    y_peer = place(x, 1 - y, z, core)
    core_peer = place(x, y, z, 1 - core)
    half_peer = {"expert": 1 - half}

    barrier = pltpu.get_barrier_semaphore()
    ahead = [z < p for p in z_at] + [y == 0, core == 1, half == 0]
    others = z_peers + [y_peer, core_peer, half_peer]
    for peer in x_peers:
        pl.semaphore_signal(barrier, inc=1, device_id=peer, device_id_type=MESH)
    for first, peer in zip(ahead, others):
        @pl.when(first)
        def _():
            pl.semaphore_signal(barrier, inc=1, device_id=peer, device_id_type=MESH)

    step_copy = pltpu.make_async_copy(ts_in, ts, weight_sems.at[2])
    step_copy.start()
    time_copy = pltpu.make_async_copy(tw_in, tw, weight_sems.at[0])
    time_copy.start()
    gate_copy = pltpu.make_async_copy(gw_in, gw, weight_sems.at[1])
    gate_copy.start()

    used = [0]

    def begin(moves):
        copies = []
        for source, target, peer in moves:
            slot = used[0]
            used[0] += 1
            copy = pltpu.make_async_remote_copy(
                src_ref=source,
                dst_ref=target,
                send_sem=send_sems.at[slot],
                recv_sem=recv_sems.at[slot],
                device_id=peer,
                device_id_type=MESH,
            )
            copy.start()
            copies.append(copy)
        return copies

    def exchange(moves):
        for copy in begin(moves):
            copy.wait()

    pl.semaphore_wait(barrier, 3 + z + y + (1 - core) + half)
    sources = (q_in, k_in, v_in, c_in)

    def send_part(head, which):
        source = sources[which]
        target = buf.at[head, which, pl.ds(pl.multiple_of(x * ROWS, ROWS), ROWS), :]
        for to, peer in zip(x_at, x_peers):
            pltpu.make_async_remote_copy(
                src_ref=source.at[:, pl.ds(pl.multiple_of((to * OWN + head) * HEAD, HEAD), HEAD)],
                dst_ref=target,
                send_sem=in_send,
                recv_sem=in_recv.at[head],
                device_id=peer,
                device_id_type=MESH,
            ).start()
        pltpu.make_async_copy(
            source.at[:, pl.ds(pl.multiple_of((x * OWN + head) * HEAD, HEAD), HEAD)],
            target,
            in_recv.at[head],
        ).start()

    def send_head(head, carry):
        for which in range(4):
            send_part(head, which)
        return carry

    send_part(0, 0)
    for first, peer in zip(ahead, others):
        @pl.when(jnp.logical_not(first))
        def _():
            pl.semaphore_signal(ready, inc=1, device_id=peer, device_id_type=MESH)

    row = lax.broadcasted_iota(jnp.int32, (NOWN, HEAD), 0)
    lane = lax.broadcasted_iota(jnp.int32, (NOWN, HEAD), 1)
    steps = jnp.zeros((NOWN, HEAD), jnp.int32)
    chosen = jnp.zeros((NOWN, HEAD), F32)
    rank = jnp.int32(0)
    step_copy.wait()
    for clip in range(NCLIP):
        own = (ts[clip] >= BOUNDARY).astype(jnp.int32) == half
        hit = row == jnp.where(own, rank, -1)
        steps = jnp.where(hit, ts[clip], steps)
        chosen = jnp.where(hit & (lane == clip), 1.0, chosen)
        rank = rank + jnp.where(own, 1, 0)
    pick_clip[...] = chosen.astype(BF16)

    frequency = jnp.exp(-math.log(10000.0) * lane.astype(F32) / (FREQ // 2))
    angles = steps.astype(F32) * frequency
    sins[:, 0:HEAD] = jnp.cos(angles)
    sins[:, HEAD:FREQ] = jnp.sin(angles)
    time_copy.wait()
    emb_cols = exact_dot(sins[...], tw[...], NT)
    own_emb[...] = jnp.zeros(own_emb.shape, F32)
    own_emb[:, 0:EMB] = emb_cols
    emb[x, y, z, core] = own_emb[...].astype(BF16)

    first = begin([(emb.at[x, y, z, core], emb.at[x, y, z, core], peer) for peer in x_peers])
    for which in range(1, 4):
        send_part(0, which)
    lax.fori_loop(1, OWN, send_head, 0)

    for copy in first:
        copy.wait()
    later = (3 - z) + (1 - y) + core + (1 - half)

    @pl.when(later > 0)
    def _():
        pl.semaphore_wait(ready, later)

    exchange([(emb.at[:, y, z, core], emb.at[:, y, z, core], y_peer)])
    exchange([(emb.at[:, :, z, core], emb.at[:, :, z, core], peer) for peer in z_peers])
    exchange([(emb.at[:, :, :, core], emb.at[:, :, :, core], core_peer)])

    def activate(group, carry):
        x_, y_ = lax.div(group, 2), lax.rem(group, 2)
        blocks = [emb[x_, y_, j // 2, j % 2].astype(F32)[:, 0:EMB] for j in range(8)]
        value = jnp.concatenate(blocks, axis=1)
        value = value / (1.0 + jnp.exp(-value))
        act[:, pl.ds(pl.multiple_of(group * GROUP, GROUP), GROUP)] = value.astype(BF16)
        return carry

    lax.fori_loop(0, 8, activate, 0)
    gate_copy.wait()
    gate_cols = dot(gw[...], act[...], NT).astype(BF16)
    cols[...] = dot(gate_cols, pick_clip[...])
    exchange([(cols, cols_in, half_peer)])
    table[y, z, core] = cols[...] + cols_in[...]
    exchange([(table.at[y, z, core], table.at[y, z, core], peer) for peer in z_peers])
    exchange([(table.at[y, :, core], table.at[y, :, core], y_peer)])
    exchange([(table.at[:, :, core], table.at[:, :, core], core_peer)])
    whole = table[...].reshape(OWN * HEAD, HEAD)
    for head in range(OWN):
        gate_rows[head] = whole[head * HEAD : (head + 1) * HEAD].T
    clip_index = half * 16 + plane

    scaling = HEAD ** (-0.5)
    dg_own[...] = jnp.zeros(dg_own.shape, F32)

    def attend(head):
        pltpu.make_async_copy(buf.at[head], buf.at[head], in_recv.at[head]).wait()
        keys = buf[head, 1]
        values = buf[head, 2]
        key_t[...] = keys.T
        value_t[...] = values.T
        gate = gate_rows[head, pl.ds(clip_index, 1), :]
        key_acc[...] = jnp.zeros(key_acc.shape, F32)
        value_acc[...] = jnp.zeros(value_acc.shape, F32)

        def block(step, d_gate):
            rows = pl.ds(pl.multiple_of(step * QB, QB), QB)
            queries = buf[head, 0, rows, :]
            scores = dot(buf[head, 1], queries, NT)
            top = jnp.max(scores, axis=0, keepdims=True)
            expo = jnp.exp2((scores - top) * (scaling * math.log2(math.e)))
            probability = expo * (1.0 / jnp.sum(expo, axis=0, keepdims=True))
            prob_half = probability.astype(BF16)
            attended = dot(value_t[...], prob_half).T.astype(BF16).astype(F32)
            cotangent = buf[head, 3, rows, :].astype(F32)
            ost[head, 0, rows, :] = (gate * attended).astype(BF16)
            d_attended = (cotangent * gate).astype(BF16)
            delta = jnp.sum((d_attended.astype(F32) * attended).T, axis=0, keepdims=True)
            d_prob = dot(buf[head, 2], d_attended, NT)
            d_scores = (probability * (d_prob - delta)).astype(BF16)
            key_acc[...] += dot(d_scores, queries)
            value_acc[...] += dot(prob_half, d_attended)
            d_query = dot(key_t[...], d_scores).T * scaling
            ost[head, 1, rows, :] = d_query.astype(BF16)
            return d_gate + jnp.sum(cotangent * attended, axis=0, keepdims=True)

        d_gate = lax.fori_loop(0, CLIP // QB, block, jnp.zeros((1, HEAD), F32))
        ost[head, 2] = (key_acc[...] * scaling).astype(BF16)
        ost[head, 3] = value_acc[...].astype(BF16)
        dg_own[pl.ds(head, 1), :] = d_gate

    targets = (gated, query_grad, key_grad, value_grad)

    def send_out(head):
        at = pl.ds(pl.multiple_of((x * OWN + head) * HEAD, HEAD), HEAD)
        for which, target in enumerate(targets):
            for to, peer in zip(x_at, x_peers):
                pltpu.make_async_remote_copy(
                    src_ref=ost.at[head, which, pl.ds(pl.multiple_of(to * ROWS, ROWS), ROWS), :],
                    dst_ref=target.at[:, at],
                    send_sem=out_send,
                    recv_sem=out_recv.at[which],
                    device_id=peer,
                    device_id_type=MESH,
                ).start()
            pltpu.make_async_copy(
                ost.at[head, which, pl.ds(pl.multiple_of(x * ROWS, ROWS), ROWS), :],
                target.at[:, at],
                out_recv.at[which],
            ).start()

    def run_head(head, carry):
        attend(head)
        send_out(head)
        return carry

    lax.fori_loop(0, OWN - 1, run_head, 0)
    attend(OWN - 1)

    dg_all[half, y, z, core] = dg_own[...]
    exchange([(dg_all.at[half, y, z, core], dg_all.at[half, y, z, core], peer) for peer in z_peers])
    exchange([(dg_all.at[half, y, :, core], dg_all.at[half, y, :, core], y_peer)])
    exchange([(dg_all.at[half, :, :, core], dg_all.at[half, :, :, core], core_peer)])
    exchange([(dg_all.at[half], dg_all.at[half], half_peer)])
    everything = dg_all[...].reshape(NCLIP, 8, HEAD)
    d_rows = jnp.zeros((NOWN, COLS), F32)
    d_cols = jnp.zeros((COLS, NOWN), F32)
    pick_row = lax.broadcasted_iota(jnp.int32, (COLS, HEAD), 0) + plane * COLS
    pick_lane = lax.broadcasted_iota(jnp.int32, (COLS, HEAD), 1)
    for head in range(OWN):
        pick = (pick_row == pick_lane + head * HEAD).astype(F32).astype(BF16)
        for part in split3(everything[:, head, :]):
            part = dot(pick_clip[:, 0:NCLIP], part).astype(BF16)
            d_rows = d_rows + dot(part, pick, NT)
            d_cols = d_cols + dot(pick, part, NT)
    row_parts = split3(d_rows)
    col_parts = split3(d_cols)
    parts[...] = jnp.zeros(parts.shape, F32)

    def weight_group(group, carry):
        at = pl.ds(pl.multiple_of(group * GROUP, GROUP), GROUP)
        weights = gw[:, at]
        value = dot(row_parts[0], weights) + (dot(row_parts[1], weights) + dot(row_parts[2], weights))
        for j in range(8):
            parts[lax.div(group, 2), lax.rem(group, 2), j // 2, j % 2, :, 0:EMB] = value[
                :, j * EMB : (j + 1) * EMB
            ]
        return carry

    lax.fori_loop(0, 8, weight_group, 0)

    copies = begin([(parts.at[:, :, :, 1 - core], in_core, core_peer)])

    def grad_group(group, carry):
        at = pl.ds(pl.multiple_of(group * GROUP, GROUP), GROUP)
        a = act[:, at]
        gate_grad[:, at] = dot(col_parts[0], a) + (dot(col_parts[1], a) + dot(col_parts[2], a))
        return carry

    lax.fori_loop(0, 8, grad_group, 0)

    copies[0].wait()
    sum_core[...] = parts[:, :, :, core] + in_core[...]
    exchange([(sum_core.at[:, :, p], in_z.at[d], peer) for d, (p, peer) in enumerate(zip(z_at, z_peers))])
    sum_z[...] = sum_core[:, :, z] + ((in_z[0] + in_z[1]) + in_z[2])
    exchange([(sum_z.at[:, 1 - y], in_y, y_peer)])
    sum_y[...] = sum_z[:, y] + in_y[...]
    half_sums[...] = sum_y[...].astype(BF16)
    copies = begin([(half_sums.at[p], in_x.at[d], peer) for d, (p, peer) in enumerate(zip(x_at, x_peers))])
    send_out(OWN - 1)
    for copy in copies:
        copy.wait()
    d_act = sum_y[x] + ((in_x[0].astype(F32) + in_x[1].astype(F32)) + in_x[2].astype(F32))
    value = emb[x, y, z, core].astype(F32)
    sigmoid = 1.0 / (1.0 + jnp.exp(-value))
    d_emb = d_act * sigmoid * (1.0 + value * (1.0 - sigmoid))
    d_emb = jnp.concatenate([d_emb, jnp.zeros((HEAD - NOWN, HEAD), F32)], axis=0).T
    result = lax.dot_general(
        d_emb[0:EMB, 0:NOWN], sins[...], NN,
        precision=lax.Precision.HIGHEST, preferred_element_type=F32,
    )
    time_grad[...] = result

    sent = buf.at[:, :, pl.ds(0, CLIP - ROWS), :]
    pltpu.make_async_copy(sent, sent, in_send).wait()
    sent = ost.at[:, :, pl.ds(0, CLIP - ROWS), :]
    pltpu.make_async_copy(sent, sent, out_send).wait()
    for which, target in enumerate(targets):
        pltpu.make_async_copy(target, target, out_recv.at[which]).wait()


def deliver(*refs):
    count = len(refs) // 2
    sems = refs[-1]
    copies = [
        pltpu.make_async_copy(refs[i], refs[count + i], sems.at[i]) for i in range(count)
    ]
    for copy in copies:
        copy.start()
    for copy in copies:
        copy.wait()


def per_device(query_rows, key_rows, value_rows, timestep, time_weight, gate_weight, cotangent):
    hbm = pl.BlockSpec(memory_space=pltpu.HBM)
    vmem = pl.BlockSpec(memory_space=pltpu.VMEM)
    blocks = (SPAN, 2, 4, 2)
    shapes = [((ROWS, DH), BF16)] * 4 + [((EMB, FREQ), F32), ((COLS, D), F32)]
    outs = pl.pallas_call(
        kernel,
        out_shape=tuple(pltpu.VMEM(shape, dtype) for shape, dtype in shapes),
        in_specs=[hbm] * 7,
        out_specs=(vmem,) * 6,
        scratch_shapes=[
            pltpu.SMEM((NCLIP,), jnp.int32),
            pltpu.VMEM((EMB, FREQ), BF16),
            pltpu.VMEM((COLS, D), BF16),
            pltpu.VMEM((OWN, 4, CLIP, HEAD), BF16),
            pltpu.VMEM((OWN, 4, CLIP, HEAD), BF16),
            pltpu.VMEM(blocks + (NOWN, HEAD), BF16),
            pltpu.VMEM((NOWN, HEAD), F32),
            pltpu.VMEM((NOWN, D), BF16),
            pltpu.VMEM((NOWN, FREQ), F32),
            pltpu.VMEM((COLS, HEAD), F32),
            pltpu.VMEM((COLS, HEAD), F32),
            pltpu.VMEM(blocks[1:] + (COLS, HEAD), F32),
            pltpu.VMEM((OWN, HEAD, HEAD), F32),
            pltpu.VMEM((8, HEAD), F32),
            pltpu.VMEM((2,) + blocks[1:] + (8, HEAD), F32),
            pltpu.VMEM(blocks + (NOWN, HEAD), F32),
            pltpu.VMEM(blocks[:3] + (NOWN, HEAD), F32),
            pltpu.VMEM(blocks[:2] + (NOWN, HEAD), F32),
            pltpu.VMEM(blocks[:1] + (NOWN, HEAD), F32),
            pltpu.VMEM(blocks[:3] + (NOWN, HEAD), F32),
            pltpu.VMEM((3,) + blocks[:2] + (NOWN, HEAD), F32),
            pltpu.VMEM(blocks[:1] + (NOWN, HEAD), F32),
            pltpu.VMEM((3, NOWN, HEAD), BF16),
            pltpu.VMEM((SPAN, NOWN, HEAD), BF16),
            pltpu.VMEM((NOWN, HEAD), BF16),
            pltpu.VMEM((HEAD, CLIP), BF16),
            pltpu.VMEM((HEAD, CLIP), BF16),
            pltpu.VMEM((CLIP, HEAD), F32),
            pltpu.VMEM((CLIP, HEAD), F32),
            pltpu.SemaphoreType.REGULAR,
            pltpu.SemaphoreType.DMA((3,)),
            pltpu.SemaphoreType.DMA((28,)),
            pltpu.SemaphoreType.DMA((28,)),
            pltpu.SemaphoreType.DMA,
            pltpu.SemaphoreType.DMA((OWN,)),
            pltpu.SemaphoreType.DMA,
            pltpu.SemaphoreType.DMA((4,)),
        ],
        compiler_params=pltpu.CompilerParams(
            collective_id=0, has_side_effects=True, vmem_limit_bytes=40 * 2**20
        ),
    )(
        *[
            pltpu.with_memory_space_constraint(array, pltpu.HBM)
            for array in (
                timestep, query_rows, key_rows, value_rows, cotangent,
                time_weight[0].T, gate_weight[0].T,
            )
        ],
    )
    outs = [pltpu.with_memory_space_constraint(out, pltpu.VMEM) for out in outs]
    outs = pl.pallas_call(
        deliver,
        out_shape=tuple(jax.ShapeDtypeStruct(shape, dtype) for shape, dtype in shapes),
        in_specs=[vmem] * 6,
        out_specs=(hbm,) * 6,
        scratch_shapes=[pltpu.SemaphoreType.DMA((6,))],
        compiler_params=pltpu.CompilerParams(vmem_limit_bytes=4 * 2**20),
    )(*outs)
    gated, query_grad, key_grad, value_grad, time_grad, gate_grad = outs
    return gated, query_grad, key_grad, value_grad, time_grad.T[None], gate_grad.T[None]


def solution(mesh):
    return jax.shard_map(
        per_device,
        mesh=mesh,
        in_specs=(
            P(("expert", "fsdp"), None),
            P(("expert", "fsdp"), None),
            P(("expert", "fsdp"), None),
            P(),
            P("expert", None, "fsdp"),
            P("expert", None, "fsdp"),
            P(("expert", "fsdp"), None),
        ),
        out_specs=(
            P(("expert", "fsdp"), None),
            P(("expert", "fsdp"), None),
            P(("expert", "fsdp"), None),
            P(("expert", "fsdp"), None),
            P("expert", None, "fsdp"),
            P("expert", None, "fsdp"),
        ),
        check_vma=False,
    )
```

```python
import math

import jax
import jax.numpy as jnp
from jax import lax
from jax.experimental import pallas as pl
from jax.experimental.pallas import tpu as pltpu
from jax.sharding import PartitionSpec as P

FREQ = 256
HEAD = 128
BOUNDARY = 875
SPAN = 4
ROWS = 256
OWN = 5
CLIP = SPAN * ROWS
NCLIP = 32
NOWN = 16
EMB = 80
COLS = 40
D = 5120
DH = 2560
GROUP = 8 * EMB
QB = 256
MESH = pl.DeviceIdType.MESH
F32 = jnp.float32
BF16 = jnp.bfloat16
NT = (((1,), (1,)), ((), ()))
NN = (((1,), (0,)), ((), ()))


def dot(a, b, dims=NN):
    return lax.dot_general(a, b, dims, preferred_element_type=F32)


def split3(value):
    high = value.astype(BF16)
    rest = value - high.astype(F32)
    middle = rest.astype(BF16)
    return high, middle, (rest - middle.astype(F32)).astype(BF16)


def exact_dot(a, b, dims=NN):
    parts = split3(a)
    return dot(parts[0], b, dims) + (dot(parts[1], b, dims) + dot(parts[2], b, dims))


def kernel(
    ts_in, q_in, k_in, v_in, c_in, tw_in, gw_in,
    gated, query_grad, key_grad, value_grad, time_grad, gate_grad,
    ts, tw, gw, buf, ost, emb, own_emb, act, sins, cols, cols_in, table, gate_rows,
    dg_own, dg_all, parts, sum_core, sum_z, sum_y, in_core, in_z, in_y, in_x, half_sums, pick_clip,
    key_t, value_t, key_acc, value_acc,
    ready, weight_sems, send_sems, recv_sems, in_send, in_recv, out_send, out_recv,
):
    half = lax.axis_index("expert")
    fsdp = lax.axis_index("fsdp")
    core = lax.rem(fsdp, 2)
    z = lax.rem(lax.div(fsdp, 2), 4)
    y = lax.rem(lax.div(fsdp, 8), 2)
    x = lax.div(fsdp, 16)
    plane = lax.rem(fsdp, 16)

    def place(x_, y_, z_, core_):
        return {"fsdp": x_ * 16 + y_ * 8 + z_ * 2 + core_}

    x_at = [lax.rem(x + d, 4) for d in (1, 2, 3)]
    z_at = [lax.rem(z + d, 4) for d in (1, 2, 3)]
    x_peers = [place(p, y, z, core) for p in x_at]
    z_peers = [place(x, y, p, core) for p in z_at]
    y_peer = place(x, 1 - y, z, core)
    core_peer = place(x, y, z, 1 - core)
    half_peer = {"expert": 1 - half}

    barrier = pltpu.get_barrier_semaphore()
    ahead = [z < p for p in z_at] + [y == 0, core == 1, half == 0]
    others = z_peers + [y_peer, core_peer, half_peer]
    for peer in x_peers:
        pl.semaphore_signal(barrier, inc=1, device_id=peer, device_id_type=MESH)
    for first, peer in zip(ahead, others):
        @pl.when(first)
        def _():
            pl.semaphore_signal(barrier, inc=1, device_id=peer, device_id_type=MESH)

    step_copy = pltpu.make_async_copy(ts_in, ts, weight_sems.at[2])
    step_copy.start()
    time_copies = [
        pltpu.make_async_copy(
            tw_in.at[:, i * HEAD : (i + 1) * HEAD], tw.at[:, i * HEAD : (i + 1) * HEAD], weight_sems.at[3 * i]
        )
        for i in range(FREQ // HEAD)
    ]
    for copy in time_copies:
        copy.start()
    gate_copy = pltpu.make_async_copy(gw_in, gw, weight_sems.at[1])
    gate_copy.start()

    used = [0]

    def begin(moves):
        copies = []
        for source, target, peer in moves:
            slot = used[0]
            used[0] += 1
            copy = pltpu.make_async_remote_copy(
                src_ref=source,
                dst_ref=target,
                send_sem=send_sems.at[slot],
                recv_sem=recv_sems.at[slot],
                device_id=peer,
                device_id_type=MESH,
            )
            copy.start()
            copies.append(copy)
        return copies

    def exchange(moves):
        for copy in begin(moves):
            copy.wait()

    pl.semaphore_wait(barrier, 3 + z + y + (1 - core) + half)
    sources = (q_in, k_in, v_in, c_in)

    def send_part(head, which):
        source = sources[which]
        target = buf.at[head, which, pl.ds(pl.multiple_of(x * ROWS, ROWS), ROWS), :]
        for to, peer in zip(x_at, x_peers):
            pltpu.make_async_remote_copy(
                src_ref=source.at[:, pl.ds(pl.multiple_of((to * OWN + head) * HEAD, HEAD), HEAD)],
                dst_ref=target,
                send_sem=in_send,
                recv_sem=in_recv.at[head],
                device_id=peer,
                device_id_type=MESH,
            ).start()
        pltpu.make_async_copy(
            source.at[:, pl.ds(pl.multiple_of((x * OWN + head) * HEAD, HEAD), HEAD)],
            target,
            in_recv.at[head],
        ).start()

    def send_head(head, carry):
        for which in range(4):
            send_part(head, which)
        return carry

    send_part(0, 0)
    for first, peer in zip(ahead, others):
        @pl.when(jnp.logical_not(first))
        def _():
            pl.semaphore_signal(ready, inc=1, device_id=peer, device_id_type=MESH)

    row = lax.broadcasted_iota(jnp.int32, (NOWN, HEAD), 0)
    lane = lax.broadcasted_iota(jnp.int32, (NOWN, HEAD), 1)
    steps = jnp.zeros((NOWN, HEAD), jnp.int32)
    chosen = jnp.zeros((NOWN, HEAD), F32)
    rank = jnp.int32(0)
    step_copy.wait()
    for clip in range(NCLIP):
        own = (ts[clip] >= BOUNDARY).astype(jnp.int32) == half
        hit = row == jnp.where(own, rank, -1)
        steps = jnp.where(hit, ts[clip], steps)
        chosen = jnp.where(hit & (lane == clip), 1.0, chosen)
        rank = rank + jnp.where(own, 1, 0)
    pick_clip[...] = chosen.astype(BF16)

    frequency = jnp.exp(-math.log(10000.0) * lane.astype(F32) / (FREQ // 2))
    angles = steps.astype(F32) * frequency
    sins[:, 0:HEAD] = jnp.cos(angles)
    sins[:, HEAD:FREQ] = jnp.sin(angles)
    for copy in time_copies:
        copy.wait()
    emb_cols = exact_dot(sins[...], tw[...], NT)
    own_emb[...] = jnp.zeros(own_emb.shape, F32)
    own_emb[:, 0:EMB] = emb_cols
    emb[x, y, z, core] = own_emb[...].astype(BF16)

    first = begin([(emb.at[x, y, z, core], emb.at[x, y, z, core], peer) for peer in x_peers])
    for which in range(1, 4):
        send_part(0, which)
    lax.fori_loop(1, OWN, send_head, 0)

    for copy in first:
        copy.wait()
    later = (3 - z) + (1 - y) + core + (1 - half)

    @pl.when(later > 0)
    def _():
        pl.semaphore_wait(ready, later)

    exchange([(emb.at[:, y, z, core], emb.at[:, y, z, core], y_peer)])
    exchange([(emb.at[:, :, z, core], emb.at[:, :, z, core], peer) for peer in z_peers])
    exchange([(emb.at[:, :, :, core], emb.at[:, :, :, core], core_peer)])

    def activate(group, carry):
        x_, y_ = lax.div(group, 2), lax.rem(group, 2)
        blocks = [emb[x_, y_, j // 2, j % 2].astype(F32)[:, 0:EMB] for j in range(8)]
        value = jnp.concatenate(blocks, axis=1)
        value = value / (1.0 + jnp.exp(-value))
        act[:, pl.ds(pl.multiple_of(group * GROUP, GROUP), GROUP)] = value.astype(BF16)
        return carry

    lax.fori_loop(0, 8, activate, 0)
    gate_copy.wait()
    gate_cols = dot(gw[...], act[...], NT).astype(BF16)
    cols[...] = dot(gate_cols, pick_clip[...])
    exchange([(cols, cols_in, half_peer)])
    table[y, z, core] = cols[...] + cols_in[...]
    exchange([(table.at[y, z, core], table.at[y, z, core], peer) for peer in z_peers])
    exchange([(table.at[y, :, core], table.at[y, :, core], y_peer)])
    exchange([(table.at[:, :, core], table.at[:, :, core], core_peer)])
    whole = table[...].reshape(OWN * HEAD, HEAD)
    for head in range(OWN):
        gate_rows[head] = whole[head * HEAD : (head + 1) * HEAD].T
    clip_index = half * 16 + plane

    scaling = HEAD ** (-0.5)
    dg_own[...] = jnp.zeros(dg_own.shape, F32)

    def attend(head):
        pltpu.make_async_copy(buf.at[head], buf.at[head], in_recv.at[head]).wait()
        keys = buf[head, 1]
        values = buf[head, 2]
        key_t[...] = keys.T
        value_t[...] = values.T
        gate = gate_rows[head, pl.ds(clip_index, 1), :]
        key_acc[...] = jnp.zeros(key_acc.shape, F32)
        value_acc[...] = jnp.zeros(value_acc.shape, F32)

        def block(step, d_gate):
            rows = pl.ds(pl.multiple_of(step * QB, QB), QB)
            queries = buf[head, 0, rows, :]
            scores = dot(buf[head, 1], queries, NT)
            top = jnp.max(scores, axis=0, keepdims=True)
            expo = jnp.exp2((scores - top) * (scaling * math.log2(math.e)))
            probability = expo * (1.0 / jnp.sum(expo, axis=0, keepdims=True))
            prob_half = probability.astype(BF16)
            attended = dot(value_t[...], prob_half).T.astype(BF16).astype(F32)
            cotangent = buf[head, 3, rows, :].astype(F32)
            ost[head, 0, rows, :] = (gate * attended).astype(BF16)
            d_attended = (cotangent * gate).astype(BF16)
            delta = jnp.sum((d_attended.astype(F32) * attended).T, axis=0, keepdims=True)
            d_prob = dot(buf[head, 2], d_attended, NT)
            d_scores = (probability * (d_prob - delta)).astype(BF16)
            key_acc[...] += dot(d_scores, queries)
            value_acc[...] += dot(prob_half, d_attended)
            d_query = dot(key_t[...], d_scores).T * scaling
            ost[head, 1, rows, :] = d_query.astype(BF16)
            return d_gate + jnp.sum(cotangent * attended, axis=0, keepdims=True)

        d_gate = lax.fori_loop(0, CLIP // QB, block, jnp.zeros((1, HEAD), F32))
        ost[head, 2] = (key_acc[...] * scaling).astype(BF16)
        ost[head, 3] = value_acc[...].astype(BF16)
        dg_own[pl.ds(head, 1), :] = d_gate

    targets = (gated, query_grad, key_grad, value_grad)

    def send_out(head):
        at = pl.ds(pl.multiple_of((x * OWN + head) * HEAD, HEAD), HEAD)
        for which, target in enumerate(targets):
            for to, peer in zip(x_at, x_peers):
                pltpu.make_async_remote_copy(
                    src_ref=ost.at[head, which, pl.ds(pl.multiple_of(to * ROWS, ROWS), ROWS), :],
                    dst_ref=target.at[:, at],
                    send_sem=out_send,
                    recv_sem=out_recv.at[which],
                    device_id=peer,
                    device_id_type=MESH,
                ).start()
            pltpu.make_async_copy(
                ost.at[head, which, pl.ds(pl.multiple_of(x * ROWS, ROWS), ROWS), :],
                target.at[:, at],
                out_recv.at[which],
            ).start()

    def run_head(head, carry):
        attend(head)
        send_out(head)
        return carry

    lax.fori_loop(0, OWN - 1, run_head, 0)
    attend(OWN - 1)

    dg_all[half, y, z, core] = dg_own[...]
    exchange([(dg_all.at[half, y, z, core], dg_all.at[half, y, z, core], peer) for peer in z_peers])
    exchange([(dg_all.at[half, y, :, core], dg_all.at[half, y, :, core], y_peer)])
    exchange([(dg_all.at[half, :, :, core], dg_all.at[half, :, :, core], core_peer)])
    exchange([(dg_all.at[half], dg_all.at[half], half_peer)])
    everything = dg_all[...].reshape(NCLIP, 8, HEAD)
    d_rows = jnp.zeros((NOWN, COLS), F32)
    d_cols = jnp.zeros((COLS, NOWN), F32)
    pick_row = lax.broadcasted_iota(jnp.int32, (COLS, HEAD), 0) + plane * COLS
    pick_lane = lax.broadcasted_iota(jnp.int32, (COLS, HEAD), 1)
    for head in range(OWN):
        pick = (pick_row == pick_lane + head * HEAD).astype(F32).astype(BF16)
        for part in split3(everything[:, head, :]):
            part = dot(pick_clip[:, 0:NCLIP], part).astype(BF16)
            d_rows = d_rows + dot(part, pick, NT)
            d_cols = d_cols + dot(pick, part, NT)
    row_parts = split3(d_rows)
    col_parts = split3(d_cols)
    parts[...] = jnp.zeros(parts.shape, F32)

    def weight_group(group, carry):
        at = pl.ds(pl.multiple_of(group * GROUP, GROUP), GROUP)
        weights = gw[:, at]
        value = dot(row_parts[0], weights) + (dot(row_parts[1], weights) + dot(row_parts[2], weights))
        for j in range(8):
            parts[lax.div(group, 2), lax.rem(group, 2), j // 2, j % 2, :, 0:EMB] = value[
                :, j * EMB : (j + 1) * EMB
            ]
        return carry

    lax.fori_loop(0, 8, weight_group, 0)

    copies = begin([(parts.at[:, :, :, 1 - core], in_core, core_peer)])

    def grad_group(group, carry):
        at = pl.ds(pl.multiple_of(group * GROUP, GROUP), GROUP)
        a = act[:, at]
        gate_grad[:, at] = dot(col_parts[0], a) + (dot(col_parts[1], a) + dot(col_parts[2], a))
        return carry

    lax.fori_loop(0, 8, grad_group, 0)

    copies[0].wait()
    sum_core[...] = parts[:, :, :, core] + in_core[...]
    exchange([(sum_core.at[:, :, p], in_z.at[d], peer) for d, (p, peer) in enumerate(zip(z_at, z_peers))])
    sum_z[...] = sum_core[:, :, z] + ((in_z[0] + in_z[1]) + in_z[2])
    exchange([(sum_z.at[:, 1 - y], in_y, y_peer)])
    sum_y[...] = sum_z[:, y] + in_y[...]
    half_sums[...] = sum_y[...].astype(BF16)
    copies = begin([(half_sums.at[p], in_x.at[d], peer) for d, (p, peer) in enumerate(zip(x_at, x_peers))])
    send_out(OWN - 1)
    for copy in copies:
        copy.wait()
    d_act = sum_y[x] + ((in_x[0].astype(F32) + in_x[1].astype(F32)) + in_x[2].astype(F32))
    value = emb[x, y, z, core].astype(F32)
    sigmoid = 1.0 / (1.0 + jnp.exp(-value))
    d_emb = d_act * sigmoid * (1.0 + value * (1.0 - sigmoid))
    d_emb = jnp.concatenate([d_emb, jnp.zeros((HEAD - NOWN, HEAD), F32)], axis=0).T
    result = lax.dot_general(
        d_emb[0:EMB, 0:NOWN], sins[...], NN,
        precision=lax.Precision.HIGHEST, preferred_element_type=F32,
    )
    time_grad[...] = result

    sent = buf.at[:, :, pl.ds(0, CLIP - ROWS), :]
    pltpu.make_async_copy(sent, sent, in_send).wait()
    sent = ost.at[:, :, pl.ds(0, CLIP - ROWS), :]
    pltpu.make_async_copy(sent, sent, out_send).wait()
    for which, target in enumerate(targets):
        pltpu.make_async_copy(target, target, out_recv.at[which]).wait()


def deliver(*refs):
    count = len(refs) // 2
    sems = refs[-1]
    copies = [
        pltpu.make_async_copy(refs[i], refs[count + i], sems.at[i]) for i in range(count)
    ]
    for copy in copies:
        copy.start()
    for copy in copies:
        copy.wait()


def per_device(query_rows, key_rows, value_rows, timestep, time_weight, gate_weight, cotangent):
    hbm = pl.BlockSpec(memory_space=pltpu.HBM)
    vmem = pl.BlockSpec(memory_space=pltpu.VMEM)
    blocks = (SPAN, 2, 4, 2)
    shapes = [((ROWS, DH), BF16)] * 4 + [((EMB, FREQ), F32), ((COLS, D), F32)]
    outs = pl.pallas_call(
        kernel,
        out_shape=tuple(pltpu.VMEM(shape, dtype) for shape, dtype in shapes),
        in_specs=[hbm] * 7,
        out_specs=(vmem,) * 6,
        scratch_shapes=[
            pltpu.SMEM((NCLIP,), jnp.int32),
            pltpu.VMEM((EMB, FREQ), BF16),
            pltpu.VMEM((COLS, D), BF16),
            pltpu.VMEM((OWN, 4, CLIP, HEAD), BF16),
            pltpu.VMEM((OWN, 4, CLIP, HEAD), BF16),
            pltpu.VMEM(blocks + (NOWN, HEAD), BF16),
            pltpu.VMEM((NOWN, HEAD), F32),
            pltpu.VMEM((NOWN, D), BF16),
            pltpu.VMEM((NOWN, FREQ), F32),
            pltpu.VMEM((COLS, HEAD), F32),
            pltpu.VMEM((COLS, HEAD), F32),
            pltpu.VMEM(blocks[1:] + (COLS, HEAD), F32),
            pltpu.VMEM((OWN, HEAD, HEAD), F32),
            pltpu.VMEM((8, HEAD), F32),
            pltpu.VMEM((2,) + blocks[1:] + (8, HEAD), F32),
            pltpu.VMEM(blocks + (NOWN, HEAD), F32),
            pltpu.VMEM(blocks[:3] + (NOWN, HEAD), F32),
            pltpu.VMEM(blocks[:2] + (NOWN, HEAD), F32),
            pltpu.VMEM(blocks[:1] + (NOWN, HEAD), F32),
            pltpu.VMEM(blocks[:3] + (NOWN, HEAD), F32),
            pltpu.VMEM((3,) + blocks[:2] + (NOWN, HEAD), F32),
            pltpu.VMEM(blocks[:1] + (NOWN, HEAD), F32),
            pltpu.VMEM((3, NOWN, HEAD), BF16),
            pltpu.VMEM((SPAN, NOWN, HEAD), BF16),
            pltpu.VMEM((NOWN, HEAD), BF16),
            pltpu.VMEM((HEAD, CLIP), BF16),
            pltpu.VMEM((HEAD, CLIP), BF16),
            pltpu.VMEM((CLIP, HEAD), F32),
            pltpu.VMEM((CLIP, HEAD), F32),
            pltpu.SemaphoreType.REGULAR,
            pltpu.SemaphoreType.DMA((4,)),
            pltpu.SemaphoreType.DMA((28,)),
            pltpu.SemaphoreType.DMA((28,)),
            pltpu.SemaphoreType.DMA,
            pltpu.SemaphoreType.DMA((OWN,)),
            pltpu.SemaphoreType.DMA,
            pltpu.SemaphoreType.DMA((4,)),
        ],
        compiler_params=pltpu.CompilerParams(
            collective_id=0, has_side_effects=True, vmem_limit_bytes=40 * 2**20
        ),
    )(
        *[
            pltpu.with_memory_space_constraint(array, pltpu.HBM)
            for array in (
                timestep, query_rows, key_rows, value_rows, cotangent,
                time_weight[0].T, gate_weight[0].T,
            )
        ],
    )
    outs = [pltpu.with_memory_space_constraint(out, pltpu.VMEM) for out in outs]
    outs = pl.pallas_call(
        deliver,
        out_shape=tuple(jax.ShapeDtypeStruct(shape, dtype) for shape, dtype in shapes),
        in_specs=[vmem] * 6,
        out_specs=(hbm,) * 6,
        scratch_shapes=[pltpu.SemaphoreType.DMA((6,))],
        compiler_params=pltpu.CompilerParams(vmem_limit_bytes=4 * 2**20),
    )(*outs)
    gated, query_grad, key_grad, value_grad, time_grad, gate_grad = outs
    return gated, query_grad, key_grad, value_grad, time_grad.T[None], gate_grad.T[None]


def solution(mesh):
    return jax.shard_map(
        per_device,
        mesh=mesh,
        in_specs=(
            P(("expert", "fsdp"), None),
            P(("expert", "fsdp"), None),
            P(("expert", "fsdp"), None),
            P(),
            P("expert", None, "fsdp"),
            P("expert", None, "fsdp"),
            P(("expert", "fsdp"), None),
        ),
        out_specs=(
            P(("expert", "fsdp"), None),
            P(("expert", "fsdp"), None),
            P(("expert", "fsdp"), None),
            P(("expert", "fsdp"), None),
            P("expert", None, "fsdp"),
            P("expert", None, "fsdp"),
        ),
        check_vma=False,
    )
```

```python
import math

import jax
import jax.numpy as jnp
from jax import lax
from jax.experimental import pallas as pl
from jax.experimental.pallas import tpu as pltpu
from jax.sharding import PartitionSpec as P

FREQ = 256
HEAD = 128
BOUNDARY = 875
SPAN = 4
ROWS = 256
OWN = 5
CLIP = SPAN * ROWS
NCLIP = 32
NOWN = 16
EMB = 80
COLS = 40
D = 5120
DH = 2560
GROUP = 8 * EMB
QB = 256
MESH = pl.DeviceIdType.MESH
F32 = jnp.float32
BF16 = jnp.bfloat16
NT = (((1,), (1,)), ((), ()))
NN = (((1,), (0,)), ((), ()))


def dot(a, b, dims=NN):
    return lax.dot_general(a, b, dims, preferred_element_type=F32)


def split3(value):
    high = value.astype(BF16)
    rest = value - high.astype(F32)
    middle = rest.astype(BF16)
    return high, middle, (rest - middle.astype(F32)).astype(BF16)


def exact_dot(a, b, dims=NN):
    parts = split3(a)
    return dot(parts[0], b, dims) + (dot(parts[1], b, dims) + dot(parts[2], b, dims))


def kernel(
    ts_in, q_in, k_in, v_in, c_in, tw_in, gw_in,
    gated, query_grad, key_grad, value_grad, time_grad, gate_grad,
    ts, tw, gw, buf, ost, emb, own_emb, act, sins, cols, cols_in, table, gate_rows,
    dg_own, dg_all, parts, sum_core, sum_z, sum_y, in_core, in_z, in_y, in_x, half_sums, pick_clip,
    key_t, value_t, key_acc, value_acc,
    ready, weight_sems, send_sems, recv_sems, in_send, in_recv, out_send, out_recv,
):
    half = lax.axis_index("expert")
    fsdp = lax.axis_index("fsdp")
    core = lax.rem(fsdp, 2)
    z = lax.rem(lax.div(fsdp, 2), 4)
    y = lax.rem(lax.div(fsdp, 8), 2)
    x = lax.div(fsdp, 16)
    plane = lax.rem(fsdp, 16)

    def place(x_, y_, z_, core_):
        return {"fsdp": x_ * 16 + y_ * 8 + z_ * 2 + core_}

    x_at = [lax.rem(x + d, 4) for d in (1, 2, 3)]
    z_at = [lax.rem(z + d, 4) for d in (1, 2, 3)]
    x_peers = [place(p, y, z, core) for p in x_at]
    z_peers = [place(x, y, p, core) for p in z_at]
    y_peer = place(x, 1 - y, z, core)
    core_peer = place(x, y, z, 1 - core)
    half_peer = {"expert": 1 - half}

    barrier = pltpu.get_barrier_semaphore()
    ahead = [z < p for p in z_at] + [y == 0, core == 1, half == 0]
    others = z_peers + [y_peer, core_peer, half_peer]
    for peer in x_peers:
        pl.semaphore_signal(barrier, inc=1, device_id=peer, device_id_type=MESH)
    for first, peer in zip(ahead, others):
        @pl.when(first)
        def _():
            pl.semaphore_signal(barrier, inc=1, device_id=peer, device_id_type=MESH)

    used = [0]

    def begin(moves):
        copies = []
        for source, target, peer in moves:
            slot = used[0]
            used[0] += 1
            copy = pltpu.make_async_remote_copy(
                src_ref=source,
                dst_ref=target,
                send_sem=send_sems.at[slot],
                recv_sem=recv_sems.at[slot],
                device_id=peer,
                device_id_type=MESH,
            )
            copy.start()
            copies.append(copy)
        return copies

    def exchange(moves):
        for copy in begin(moves):
            copy.wait()

    pl.semaphore_wait(barrier, 3 + z + y + (1 - core) + half)
    sources = (q_in, k_in, v_in, c_in)

    def send_part(head, which):
        source = sources[which]
        target = buf.at[head, which, pl.ds(pl.multiple_of(x * ROWS, ROWS), ROWS), :]
        for to, peer in zip(x_at, x_peers):
            pltpu.make_async_remote_copy(
                src_ref=source.at[:, pl.ds(pl.multiple_of((to * OWN + head) * HEAD, HEAD), HEAD)],
                dst_ref=target,
                send_sem=in_send,
                recv_sem=in_recv.at[head],
                device_id=peer,
                device_id_type=MESH,
            ).start()
        pltpu.make_async_copy(
            source.at[:, pl.ds(pl.multiple_of((x * OWN + head) * HEAD, HEAD), HEAD)],
            target,
            in_recv.at[head],
        ).start()

    def send_head(head, carry):
        for which in range(4):
            send_part(head, which)
        return carry

    send_part(0, 0)
    step_copy = pltpu.make_async_copy(ts_in, ts, weight_sems.at[2])
    step_copy.start()
    time_copies = [
        pltpu.make_async_copy(
            tw_in.at[:, i * HEAD : (i + 1) * HEAD], tw.at[:, i * HEAD : (i + 1) * HEAD], weight_sems.at[3 * i]
        )
        for i in range(FREQ // HEAD)
    ]
    for copy in time_copies:
        copy.start()
    gate_copy = pltpu.make_async_copy(gw_in, gw, weight_sems.at[1])
    gate_copy.start()
    for first, peer in zip(ahead, others):
        @pl.when(jnp.logical_not(first))
        def _():
            pl.semaphore_signal(ready, inc=1, device_id=peer, device_id_type=MESH)

    row = lax.broadcasted_iota(jnp.int32, (NOWN, HEAD), 0)
    lane = lax.broadcasted_iota(jnp.int32, (NOWN, HEAD), 1)
    steps = jnp.zeros((NOWN, HEAD), jnp.int32)
    chosen = jnp.zeros((NOWN, HEAD), F32)
    rank = jnp.int32(0)
    step_copy.wait()
    for clip in range(NCLIP):
        own = (ts[clip] >= BOUNDARY).astype(jnp.int32) == half
        hit = row == jnp.where(own, rank, -1)
        steps = jnp.where(hit, ts[clip], steps)
        chosen = jnp.where(hit & (lane == clip), 1.0, chosen)
        rank = rank + jnp.where(own, 1, 0)
    pick_clip[...] = chosen.astype(BF16)

    frequency = jnp.exp(-math.log(10000.0) * lane.astype(F32) / (FREQ // 2))
    angles = steps.astype(F32) * frequency
    sins[:, 0:HEAD] = jnp.cos(angles)
    sins[:, HEAD:FREQ] = jnp.sin(angles)
    for copy in time_copies:
        copy.wait()
    emb_cols = exact_dot(sins[...], tw[...], NT)
    own_emb[...] = jnp.zeros(own_emb.shape, F32)
    own_emb[:, 0:EMB] = emb_cols
    emb[x, y, z, core] = own_emb[...].astype(BF16)

    first = begin([(emb.at[x, y, z, core], emb.at[x, y, z, core], peer) for peer in x_peers])
    for which in range(1, 4):
        send_part(0, which)
    lax.fori_loop(1, OWN, send_head, 0)

    for copy in first:
        copy.wait()
    later = (3 - z) + (1 - y) + core + (1 - half)

    @pl.when(later > 0)
    def _():
        pl.semaphore_wait(ready, later)

    exchange([(emb.at[:, y, z, core], emb.at[:, y, z, core], y_peer)])
    exchange([(emb.at[:, :, z, core], emb.at[:, :, z, core], peer) for peer in z_peers])
    exchange([(emb.at[:, :, :, core], emb.at[:, :, :, core], core_peer)])

    def activate(group, carry):
        x_, y_ = lax.div(group, 2), lax.rem(group, 2)
        blocks = [emb[x_, y_, j // 2, j % 2].astype(F32)[:, 0:EMB] for j in range(8)]
        value = jnp.concatenate(blocks, axis=1)
        value = value / (1.0 + jnp.exp(-value))
        act[:, pl.ds(pl.multiple_of(group * GROUP, GROUP), GROUP)] = value.astype(BF16)
        return carry

    lax.fori_loop(0, 8, activate, 0)
    gate_copy.wait()
    gate_cols = dot(gw[...], act[...], NT).astype(BF16)
    cols[...] = dot(gate_cols, pick_clip[...])
    exchange([(cols, cols_in, half_peer)])
    table[y, z, core] = cols[...] + cols_in[...]
    exchange([(table.at[y, z, core], table.at[y, z, core], peer) for peer in z_peers])
    exchange([(table.at[y, :, core], table.at[y, :, core], y_peer)])
    exchange([(table.at[:, :, core], table.at[:, :, core], core_peer)])
    whole = table[...].reshape(OWN * HEAD, HEAD)
    for head in range(OWN):
        gate_rows[head] = whole[head * HEAD : (head + 1) * HEAD].T
    clip_index = half * 16 + plane

    scaling = HEAD ** (-0.5)
    dg_own[...] = jnp.zeros(dg_own.shape, F32)

    def attend(head):
        pltpu.make_async_copy(buf.at[head], buf.at[head], in_recv.at[head]).wait()
        keys = buf[head, 1]
        values = buf[head, 2]
        key_t[...] = keys.T
        value_t[...] = values.T
        gate = gate_rows[head, pl.ds(clip_index, 1), :]
        key_acc[...] = jnp.zeros(key_acc.shape, F32)
        value_acc[...] = jnp.zeros(value_acc.shape, F32)

        def block(step, d_gate):
            rows = pl.ds(pl.multiple_of(step * QB, QB), QB)
            queries = buf[head, 0, rows, :]
            scores = dot(buf[head, 1], queries, NT)
            top = jnp.max(scores, axis=0, keepdims=True)
            expo = jnp.exp2((scores - top) * (scaling * math.log2(math.e)))
            probability = expo * (1.0 / jnp.sum(expo, axis=0, keepdims=True))
            prob_half = probability.astype(BF16)
            attended = dot(value_t[...], prob_half).T.astype(BF16).astype(F32)
            cotangent = buf[head, 3, rows, :].astype(F32)
            ost[head, 0, rows, :] = (gate * attended).astype(BF16)
            d_attended = (cotangent * gate).astype(BF16)
            delta = jnp.sum((d_attended.astype(F32) * attended).T, axis=0, keepdims=True)
            d_prob = dot(buf[head, 2], d_attended, NT)
            d_scores = (probability * (d_prob - delta)).astype(BF16)
            key_acc[...] += dot(d_scores, queries)
            value_acc[...] += dot(prob_half, d_attended)
            d_query = dot(key_t[...], d_scores).T * scaling
            ost[head, 1, rows, :] = d_query.astype(BF16)
            return d_gate + jnp.sum(cotangent * attended, axis=0, keepdims=True)

        d_gate = lax.fori_loop(0, CLIP // QB, block, jnp.zeros((1, HEAD), F32))
        ost[head, 2] = (key_acc[...] * scaling).astype(BF16)
        ost[head, 3] = value_acc[...].astype(BF16)
        dg_own[pl.ds(head, 1), :] = d_gate

    targets = (gated, query_grad, key_grad, value_grad)

    def send_out(head):
        at = pl.ds(pl.multiple_of((x * OWN + head) * HEAD, HEAD), HEAD)
        for which, target in enumerate(targets):
            for to, peer in zip(x_at, x_peers):
                pltpu.make_async_remote_copy(
                    src_ref=ost.at[head, which, pl.ds(pl.multiple_of(to * ROWS, ROWS), ROWS), :],
                    dst_ref=target.at[:, at],
                    send_sem=out_send,
                    recv_sem=out_recv.at[which],
                    device_id=peer,
                    device_id_type=MESH,
                ).start()
            pltpu.make_async_copy(
                ost.at[head, which, pl.ds(pl.multiple_of(x * ROWS, ROWS), ROWS), :],
                target.at[:, at],
                out_recv.at[which],
            ).start()

    def run_head(head, carry):
        attend(head)
        send_out(head)
        return carry

    lax.fori_loop(0, OWN - 1, run_head, 0)
    attend(OWN - 1)

    dg_all[half, y, z, core] = dg_own[...]
    exchange([(dg_all.at[half, y, z, core], dg_all.at[half, y, z, core], peer) for peer in z_peers])
    exchange([(dg_all.at[half, y, :, core], dg_all.at[half, y, :, core], y_peer)])
    exchange([(dg_all.at[half, :, :, core], dg_all.at[half, :, :, core], core_peer)])
    exchange([(dg_all.at[half], dg_all.at[half], half_peer)])
    everything = dg_all[...].reshape(NCLIP, 8, HEAD)
    d_rows = jnp.zeros((NOWN, COLS), F32)
    d_cols = jnp.zeros((COLS, NOWN), F32)
    pick_row = lax.broadcasted_iota(jnp.int32, (COLS, HEAD), 0) + plane * COLS
    pick_lane = lax.broadcasted_iota(jnp.int32, (COLS, HEAD), 1)
    for head in range(OWN):
        pick = (pick_row == pick_lane + head * HEAD).astype(F32).astype(BF16)
        for part in split3(everything[:, head, :]):
            part = dot(pick_clip[:, 0:NCLIP], part).astype(BF16)
            d_rows = d_rows + dot(part, pick, NT)
            d_cols = d_cols + dot(pick, part, NT)
    row_parts = split3(d_rows)
    col_parts = split3(d_cols)
    parts[...] = jnp.zeros(parts.shape, F32)

    def weight_group(group, carry):
        at = pl.ds(pl.multiple_of(group * GROUP, GROUP), GROUP)
        weights = gw[:, at]
        value = dot(row_parts[0], weights) + (dot(row_parts[1], weights) + dot(row_parts[2], weights))
        for j in range(8):
            parts[lax.div(group, 2), lax.rem(group, 2), j // 2, j % 2, :, 0:EMB] = value[
                :, j * EMB : (j + 1) * EMB
            ]
        return carry

    lax.fori_loop(0, 8, weight_group, 0)

    copies = begin([(parts.at[:, :, :, 1 - core], in_core, core_peer)])

    def grad_group(group, carry):
        at = pl.ds(pl.multiple_of(group * GROUP, GROUP), GROUP)
        a = act[:, at]
        gate_grad[:, at] = dot(col_parts[0], a) + (dot(col_parts[1], a) + dot(col_parts[2], a))
        return carry

    lax.fori_loop(0, 8, grad_group, 0)

    copies[0].wait()
    sum_core[...] = parts[:, :, :, core] + in_core[...]
    exchange([(sum_core.at[:, :, p], in_z.at[d], peer) for d, (p, peer) in enumerate(zip(z_at, z_peers))])
    sum_z[...] = sum_core[:, :, z] + ((in_z[0] + in_z[1]) + in_z[2])
    exchange([(sum_z.at[:, 1 - y], in_y, y_peer)])
    sum_y[...] = sum_z[:, y] + in_y[...]
    half_sums[...] = sum_y[...].astype(BF16)
    copies = begin([(half_sums.at[p], in_x.at[d], peer) for d, (p, peer) in enumerate(zip(x_at, x_peers))])
    send_out(OWN - 1)
    for copy in copies:
        copy.wait()
    d_act = sum_y[x] + ((in_x[0].astype(F32) + in_x[1].astype(F32)) + in_x[2].astype(F32))
    value = emb[x, y, z, core].astype(F32)
    sigmoid = 1.0 / (1.0 + jnp.exp(-value))
    d_emb = d_act * sigmoid * (1.0 + value * (1.0 - sigmoid))
    d_emb = jnp.concatenate([d_emb, jnp.zeros((HEAD - NOWN, HEAD), F32)], axis=0).T
    result = lax.dot_general(
        d_emb[0:EMB, 0:NOWN], sins[...], NN,
        precision=lax.Precision.HIGHEST, preferred_element_type=F32,
    )
    time_grad[...] = result

    sent = buf.at[:, :, pl.ds(0, CLIP - ROWS), :]
    pltpu.make_async_copy(sent, sent, in_send).wait()
    sent = ost.at[:, :, pl.ds(0, CLIP - ROWS), :]
    pltpu.make_async_copy(sent, sent, out_send).wait()
    for which, target in enumerate(targets):
        pltpu.make_async_copy(target, target, out_recv.at[which]).wait()


def deliver(*refs):
    count = len(refs) // 2
    sems = refs[-1]
    copies = [
        pltpu.make_async_copy(refs[i], refs[count + i], sems.at[i]) for i in range(count)
    ]
    for copy in copies:
        copy.start()
    for copy in copies:
        copy.wait()


def per_device(query_rows, key_rows, value_rows, timestep, time_weight, gate_weight, cotangent):
    hbm = pl.BlockSpec(memory_space=pltpu.HBM)
    vmem = pl.BlockSpec(memory_space=pltpu.VMEM)
    blocks = (SPAN, 2, 4, 2)
    shapes = [((ROWS, DH), BF16)] * 4 + [((EMB, FREQ), F32), ((COLS, D), F32)]
    outs = pl.pallas_call(
        kernel,
        out_shape=tuple(pltpu.VMEM(shape, dtype) for shape, dtype in shapes),
        in_specs=[hbm] * 7,
        out_specs=(vmem,) * 6,
        scratch_shapes=[
            pltpu.SMEM((NCLIP,), jnp.int32),
            pltpu.VMEM((EMB, FREQ), BF16),
            pltpu.VMEM((COLS, D), BF16),
            pltpu.VMEM((OWN, 4, CLIP, HEAD), BF16),
            pltpu.VMEM((OWN, 4, CLIP, HEAD), BF16),
            pltpu.VMEM(blocks + (NOWN, HEAD), BF16),
            pltpu.VMEM((NOWN, HEAD), F32),
            pltpu.VMEM((NOWN, D), BF16),
            pltpu.VMEM((NOWN, FREQ), F32),
            pltpu.VMEM((COLS, HEAD), F32),
            pltpu.VMEM((COLS, HEAD), F32),
            pltpu.VMEM(blocks[1:] + (COLS, HEAD), F32),
            pltpu.VMEM((OWN, HEAD, HEAD), F32),
            pltpu.VMEM((8, HEAD), F32),
            pltpu.VMEM((2,) + blocks[1:] + (8, HEAD), F32),
            pltpu.VMEM(blocks + (NOWN, HEAD), F32),
            pltpu.VMEM(blocks[:3] + (NOWN, HEAD), F32),
            pltpu.VMEM(blocks[:2] + (NOWN, HEAD), F32),
            pltpu.VMEM(blocks[:1] + (NOWN, HEAD), F32),
            pltpu.VMEM(blocks[:3] + (NOWN, HEAD), F32),
            pltpu.VMEM((3,) + blocks[:2] + (NOWN, HEAD), F32),
            pltpu.VMEM(blocks[:1] + (NOWN, HEAD), F32),
            pltpu.VMEM((3, NOWN, HEAD), BF16),
            pltpu.VMEM((SPAN, NOWN, HEAD), BF16),
            pltpu.VMEM((NOWN, HEAD), BF16),
            pltpu.VMEM((HEAD, CLIP), BF16),
            pltpu.VMEM((HEAD, CLIP), BF16),
            pltpu.VMEM((CLIP, HEAD), F32),
            pltpu.VMEM((CLIP, HEAD), F32),
            pltpu.SemaphoreType.REGULAR,
            pltpu.SemaphoreType.DMA((4,)),
            pltpu.SemaphoreType.DMA((28,)),
            pltpu.SemaphoreType.DMA((28,)),
            pltpu.SemaphoreType.DMA,
            pltpu.SemaphoreType.DMA((OWN,)),
            pltpu.SemaphoreType.DMA,
            pltpu.SemaphoreType.DMA((4,)),
        ],
        compiler_params=pltpu.CompilerParams(
            collective_id=0, has_side_effects=True, vmem_limit_bytes=40 * 2**20
        ),
    )(
        *[
            pltpu.with_memory_space_constraint(array, pltpu.HBM)
            for array in (
                timestep, query_rows, key_rows, value_rows, cotangent,
                time_weight[0].T, gate_weight[0].T,
            )
        ],
    )
    outs = [pltpu.with_memory_space_constraint(out, pltpu.VMEM) for out in outs]
    outs = pl.pallas_call(
        deliver,
        out_shape=tuple(jax.ShapeDtypeStruct(shape, dtype) for shape, dtype in shapes),
        in_specs=[vmem] * 6,
        out_specs=(hbm,) * 6,
        scratch_shapes=[pltpu.SemaphoreType.DMA((6,))],
        compiler_params=pltpu.CompilerParams(vmem_limit_bytes=4 * 2**20),
    )(*outs)
    gated, query_grad, key_grad, value_grad, time_grad, gate_grad = outs
    return gated, query_grad, key_grad, value_grad, time_grad.T[None], gate_grad.T[None]


def solution(mesh):
    return jax.shard_map(
        per_device,
        mesh=mesh,
        in_specs=(
            P(("expert", "fsdp"), None),
            P(("expert", "fsdp"), None),
            P(("expert", "fsdp"), None),
            P(),
            P("expert", None, "fsdp"),
            P("expert", None, "fsdp"),
            P(("expert", "fsdp"), None),
        ),
        out_specs=(
            P(("expert", "fsdp"), None),
            P(("expert", "fsdp"), None),
            P(("expert", "fsdp"), None),
            P(("expert", "fsdp"), None),
            P("expert", None, "fsdp"),
            P("expert", None, "fsdp"),
        ),
        check_vma=False,
    )
```

```python
import math

import jax
import jax.numpy as jnp
from jax import lax
from jax.experimental import pallas as pl
from jax.experimental.pallas import tpu as pltpu
from jax.sharding import PartitionSpec as P

FREQ = 256
HEAD = 128
BOUNDARY = 875
SPAN = 4
ROWS = 256
OWN = 5
CLIP = SPAN * ROWS
NCLIP = 32
NOWN = 16
EMB = 80
COLS = 40
D = 5120
DH = 2560
GROUP = 8 * EMB
QB = 256
MESH = pl.DeviceIdType.MESH
F32 = jnp.float32
BF16 = jnp.bfloat16
NT = (((1,), (1,)), ((), ()))
NN = (((1,), (0,)), ((), ()))


def dot(a, b, dims=NN):
    return lax.dot_general(a, b, dims, preferred_element_type=F32)


def split3(value):
    high = value.astype(BF16)
    rest = value - high.astype(F32)
    middle = rest.astype(BF16)
    return high, middle, (rest - middle.astype(F32)).astype(BF16)


def exact_dot(a, b, dims=NN):
    parts = split3(a)
    return dot(parts[0], b, dims) + (dot(parts[1], b, dims) + dot(parts[2], b, dims))


def kernel(
    ts_in, q_in, k_in, v_in, c_in, tw_in, gw_in,
    gated, query_grad, key_grad, value_grad, time_grad, gate_grad,
    ts, tw, gw, buf, ost, emb, own_emb, act, sins, cols, cols_in, table, gate_rows,
    dg_own, dg_all, parts, sum_core, sum_z, sum_y, in_core, in_z, in_y, in_x, half_sums, pick_clip,
    key_t, value_t, key_acc, value_acc,
    ready, weight_sems, send_sems, recv_sems, in_send, in_recv, out_send, out_recv,
):
    half = lax.axis_index("expert")
    fsdp = lax.axis_index("fsdp")
    core = lax.rem(fsdp, 2)
    z = lax.rem(lax.div(fsdp, 2), 4)
    y = lax.rem(lax.div(fsdp, 8), 2)
    x = lax.div(fsdp, 16)
    plane = lax.rem(fsdp, 16)

    def place(x_, y_, z_, core_):
        return {"fsdp": x_ * 16 + y_ * 8 + z_ * 2 + core_}

    x_at = [lax.rem(x + d, 4) for d in (1, 2, 3)]
    z_at = [lax.rem(z + d, 4) for d in (1, 2, 3)]
    x_peers = [place(p, y, z, core) for p in x_at]
    z_peers = [place(x, y, p, core) for p in z_at]
    y_peer = place(x, 1 - y, z, core)
    core_peer = place(x, y, z, 1 - core)
    half_peer = {"expert": 1 - half}

    barrier = pltpu.get_barrier_semaphore()
    ahead = [z < p for p in z_at] + [y == 0, core == 1, half == 0]
    others = z_peers + [y_peer, core_peer, half_peer]
    for peer in x_peers:
        pl.semaphore_signal(barrier, inc=1, device_id=peer, device_id_type=MESH)
    for first, peer in zip(ahead, others):
        @pl.when(first)
        def _():
            pl.semaphore_signal(barrier, inc=1, device_id=peer, device_id_type=MESH)

    step_copy = pltpu.make_async_copy(ts_in, ts, weight_sems.at[2])
    step_copy.start()
    time_copies = [
        pltpu.make_async_copy(
            tw_in.at[:, i * HEAD : (i + 1) * HEAD], tw.at[:, i * HEAD : (i + 1) * HEAD], weight_sems.at[3 * i]
        )
        for i in range(FREQ // HEAD)
    ]
    for copy in time_copies:
        copy.start()
    gate_copy = pltpu.make_async_copy(gw_in, gw, weight_sems.at[1])
    gate_copy.start()

    used = [0]

    def begin(moves):
        copies = []
        for source, target, peer in moves:
            slot = used[0]
            used[0] += 1
            copy = pltpu.make_async_remote_copy(
                src_ref=source,
                dst_ref=target,
                send_sem=send_sems.at[slot],
                recv_sem=recv_sems.at[slot],
                device_id=peer,
                device_id_type=MESH,
            )
            copy.start()
            copies.append(copy)
        return copies

    def exchange(moves):
        for copy in begin(moves):
            copy.wait()

    pl.semaphore_wait(barrier, 3 + z + y + (1 - core) + half)
    sources = (q_in, k_in, v_in, c_in)

    def send_part(head, which):
        source = sources[which]
        target = buf.at[head, which, pl.ds(pl.multiple_of(x * ROWS, ROWS), ROWS), :]
        for to, peer in zip(x_at, x_peers):
            pltpu.make_async_remote_copy(
                src_ref=source.at[:, pl.ds(pl.multiple_of((to * OWN + head) * HEAD, HEAD), HEAD)],
                dst_ref=target,
                send_sem=in_send,
                recv_sem=in_recv.at[head],
                device_id=peer,
                device_id_type=MESH,
            ).start()
        pltpu.make_async_copy(
            source.at[:, pl.ds(pl.multiple_of((x * OWN + head) * HEAD, HEAD), HEAD)],
            target,
            in_recv.at[head],
        ).start()

    def send_head(head, carry):
        for which in range(4):
            send_part(head, which)
        return carry

    send_part(0, 0)
    for first, peer in zip(ahead, others):
        @pl.when(jnp.logical_not(first))
        def _():
            pl.semaphore_signal(ready, inc=1, device_id=peer, device_id_type=MESH)

    row = lax.broadcasted_iota(jnp.int32, (NOWN, HEAD), 0)
    lane = lax.broadcasted_iota(jnp.int32, (NOWN, HEAD), 1)
    steps = jnp.zeros((NOWN, HEAD), jnp.int32)
    chosen = jnp.zeros((NOWN, HEAD), F32)
    rank = jnp.int32(0)
    step_copy.wait()
    for clip in range(NCLIP):
        own = (ts[clip] >= BOUNDARY).astype(jnp.int32) == half
        hit = row == jnp.where(own, rank, -1)
        steps = jnp.where(hit, ts[clip], steps)
        chosen = jnp.where(hit & (lane == clip), 1.0, chosen)
        rank = rank + jnp.where(own, 1, 0)
    pick_clip[...] = chosen.astype(BF16)

    frequency = jnp.exp(-math.log(10000.0) * lane.astype(F32) / (FREQ // 2))
    angles = steps.astype(F32) * frequency
    sins[:, 0:HEAD] = jnp.cos(angles)
    sins[:, HEAD:FREQ] = jnp.sin(angles)
    for copy in time_copies:
        copy.wait()
    emb_cols = exact_dot(sins[...], tw[...], NT)
    own_emb[...] = jnp.zeros(own_emb.shape, F32)
    own_emb[:, 0:EMB] = emb_cols
    emb[x, y, z, core] = own_emb[...].astype(BF16)

    first = begin([(emb.at[x, y, z, core], emb.at[x, y, z, core], peer) for peer in x_peers])
    for which in range(1, 4):
        send_part(0, which)
    lax.fori_loop(1, OWN, send_head, 0)

    for copy in first:
        copy.wait()
    later = (3 - z) + (1 - y) + core + (1 - half)

    @pl.when(later > 0)
    def _():
        pl.semaphore_wait(ready, later)

    exchange([(emb.at[:, y, z, core], emb.at[:, y, z, core], y_peer)])
    exchange([(emb.at[:, :, z, core], emb.at[:, :, z, core], peer) for peer in z_peers])
    exchange([(emb.at[:, :, :, core], emb.at[:, :, :, core], core_peer)])

    def activate(group, carry):
        x_, y_ = lax.div(group, 2), lax.rem(group, 2)
        blocks = [emb[x_, y_, j // 2, j % 2].astype(F32)[:, 0:EMB] for j in range(8)]
        value = jnp.concatenate(blocks, axis=1)
        value = value / (1.0 + jnp.exp(-value))
        act[:, pl.ds(pl.multiple_of(group * GROUP, GROUP), GROUP)] = value.astype(BF16)
        return carry

    lax.fori_loop(0, 8, activate, 0)
    gate_copy.wait()
    gate_cols = dot(gw[...], act[...], NT).astype(BF16)
    cols[...] = dot(gate_cols, pick_clip[...])
    exchange([(cols, cols_in, half_peer)])
    table[y, z, core] = cols[...] + cols_in[...]
    exchange([(table.at[y, z, core], table.at[y, z, core], peer) for peer in z_peers])
    exchange([(table.at[y, :, core], table.at[y, :, core], y_peer)])
    exchange([(table.at[:, :, core], table.at[:, :, core], core_peer)])
    whole = table[...].reshape(OWN * HEAD, HEAD)
    for head in range(OWN):
        gate_rows[head] = whole[head * HEAD : (head + 1) * HEAD].T
    clip_index = half * 16 + plane

    scaling = HEAD ** (-0.5)
    dg_own[...] = jnp.zeros(dg_own.shape, F32)

    def attend(head):
        pltpu.make_async_copy(buf.at[head], buf.at[head], in_recv.at[head]).wait()
        keys = buf[head, 1]
        values = buf[head, 2]
        key_t[...] = keys.T
        value_t[...] = values.T
        gate = gate_rows[head, pl.ds(clip_index, 1), :]
        key_acc[...] = jnp.zeros(key_acc.shape, F32)
        value_acc[...] = jnp.zeros(value_acc.shape, F32)

        def block(step, d_gate):
            rows = pl.ds(pl.multiple_of(step * QB, QB), QB)
            queries = buf[head, 0, rows, :]
            scores = dot(buf[head, 1], queries, NT)
            top = jnp.max(scores, axis=0, keepdims=True)
            expo = jnp.exp2((scores - top) * (scaling * math.log2(math.e)))
            probability = expo * (1.0 / jnp.sum(expo, axis=0, keepdims=True))
            prob_half = probability.astype(BF16)
            attended = dot(value_t[...], prob_half).T.astype(BF16).astype(F32)
            cotangent = buf[head, 3, rows, :].astype(F32)
            ost[head, 0, rows, :] = (gate * attended).astype(BF16)
            d_attended = (cotangent * gate).astype(BF16)
            delta = jnp.sum((d_attended.astype(F32) * attended).T, axis=0, keepdims=True)
            d_prob = dot(buf[head, 2], d_attended, NT)
            d_scores = (probability * (d_prob - delta)).astype(BF16)
            key_acc[...] += dot(d_scores, queries)
            value_acc[...] += dot(prob_half, d_attended)
            d_query = dot(key_t[...], d_scores).T * scaling
            ost[head, 1, rows, :] = d_query.astype(BF16)
            return d_gate + jnp.sum(cotangent * attended, axis=0, keepdims=True)

        d_gate = lax.fori_loop(0, CLIP // QB, block, jnp.zeros((1, HEAD), F32))
        ost[head, 2] = (key_acc[...] * scaling).astype(BF16)
        ost[head, 3] = value_acc[...].astype(BF16)
        dg_own[pl.ds(head, 1), :] = d_gate

    targets = (gated, query_grad, key_grad, value_grad)

    def send_out(head, arrays=range(4)):
        at = pl.ds(pl.multiple_of((x * OWN + head) * HEAD, HEAD), HEAD)
        for which in arrays:
            target = targets[which]
            for to, peer in zip(x_at, x_peers):
                pltpu.make_async_remote_copy(
                    src_ref=ost.at[head, which, pl.ds(pl.multiple_of(to * ROWS, ROWS), ROWS), :],
                    dst_ref=target.at[:, at],
                    send_sem=out_send,
                    recv_sem=out_recv.at[which],
                    device_id=peer,
                    device_id_type=MESH,
                ).start()
            pltpu.make_async_copy(
                ost.at[head, which, pl.ds(pl.multiple_of(x * ROWS, ROWS), ROWS), :],
                target.at[:, at],
                out_recv.at[which],
            ).start()

    def run_head(head, carry):
        attend(head)
        send_out(head)
        return carry

    lax.fori_loop(0, OWN - 1, run_head, 0)
    attend(OWN - 1)
    send_out(OWN - 1, (0, 1))

    dg_all[half, y, z, core] = dg_own[...]
    exchange([(dg_all.at[half, y, z, core], dg_all.at[half, y, z, core], peer) for peer in z_peers])
    exchange([(dg_all.at[half, y, :, core], dg_all.at[half, y, :, core], y_peer)])
    exchange([(dg_all.at[half, :, :, core], dg_all.at[half, :, :, core], core_peer)])
    exchange([(dg_all.at[half], dg_all.at[half], half_peer)])
    everything = dg_all[...].reshape(NCLIP, 8, HEAD)
    d_rows = jnp.zeros((NOWN, COLS), F32)
    d_cols = jnp.zeros((COLS, NOWN), F32)
    pick_row = lax.broadcasted_iota(jnp.int32, (COLS, HEAD), 0) + plane * COLS
    pick_lane = lax.broadcasted_iota(jnp.int32, (COLS, HEAD), 1)
    for head in range(OWN):
        pick = (pick_row == pick_lane + head * HEAD).astype(F32).astype(BF16)
        for part in split3(everything[:, head, :]):
            part = dot(pick_clip[:, 0:NCLIP], part).astype(BF16)
            d_rows = d_rows + dot(part, pick, NT)
            d_cols = d_cols + dot(pick, part, NT)
    row_parts = split3(d_rows)
    col_parts = split3(d_cols)
    parts[...] = jnp.zeros(parts.shape, F32)

    def weight_group(group, carry):
        at = pl.ds(pl.multiple_of(group * GROUP, GROUP), GROUP)
        weights = gw[:, at]
        value = dot(row_parts[0], weights) + (dot(row_parts[1], weights) + dot(row_parts[2], weights))
        for j in range(8):
            parts[lax.div(group, 2), lax.rem(group, 2), j // 2, j % 2, :, 0:EMB] = value[
                :, j * EMB : (j + 1) * EMB
            ]
        return carry

    lax.fori_loop(0, 8, weight_group, 0)

    copies = begin([(parts.at[:, :, :, 1 - core], in_core, core_peer)])

    def grad_group(group, carry):
        at = pl.ds(pl.multiple_of(group * GROUP, GROUP), GROUP)
        a = act[:, at]
        gate_grad[:, at] = dot(col_parts[0], a) + (dot(col_parts[1], a) + dot(col_parts[2], a))
        return carry

    lax.fori_loop(0, 8, grad_group, 0)

    copies[0].wait()
    sum_core[...] = parts[:, :, :, core] + in_core[...]
    exchange([(sum_core.at[:, :, p], in_z.at[d], peer) for d, (p, peer) in enumerate(zip(z_at, z_peers))])
    sum_z[...] = sum_core[:, :, z] + ((in_z[0] + in_z[1]) + in_z[2])
    exchange([(sum_z.at[:, 1 - y], in_y, y_peer)])
    sum_y[...] = sum_z[:, y] + in_y[...]
    half_sums[...] = sum_y[...].astype(BF16)
    copies = begin([(half_sums.at[p], in_x.at[d], peer) for d, (p, peer) in enumerate(zip(x_at, x_peers))])
    send_out(OWN - 1, (2, 3))
    for copy in copies:
        copy.wait()
    d_act = sum_y[x] + ((in_x[0].astype(F32) + in_x[1].astype(F32)) + in_x[2].astype(F32))
    value = emb[x, y, z, core].astype(F32)
    sigmoid = 1.0 / (1.0 + jnp.exp(-value))
    d_emb = d_act * sigmoid * (1.0 + value * (1.0 - sigmoid))
    d_emb = jnp.concatenate([d_emb, jnp.zeros((HEAD - NOWN, HEAD), F32)], axis=0).T
    result = lax.dot_general(
        d_emb[0:EMB, 0:NOWN], sins[...], NN,
        precision=lax.Precision.HIGHEST, preferred_element_type=F32,
    )
    time_grad[...] = result

    sent = buf.at[:, :, pl.ds(0, CLIP - ROWS), :]
    pltpu.make_async_copy(sent, sent, in_send).wait()
    sent = ost.at[:, :, pl.ds(0, CLIP - ROWS), :]
    pltpu.make_async_copy(sent, sent, out_send).wait()
    for which, target in enumerate(targets):
        pltpu.make_async_copy(target, target, out_recv.at[which]).wait()


def deliver(*refs):
    count = len(refs) // 2
    sems = refs[-1]
    copies = [
        pltpu.make_async_copy(refs[i], refs[count + i], sems.at[i]) for i in range(count)
    ]
    for copy in copies:
        copy.start()
    for copy in copies:
        copy.wait()


def per_device(query_rows, key_rows, value_rows, timestep, time_weight, gate_weight, cotangent):
    hbm = pl.BlockSpec(memory_space=pltpu.HBM)
    vmem = pl.BlockSpec(memory_space=pltpu.VMEM)
    blocks = (SPAN, 2, 4, 2)
    shapes = [((ROWS, DH), BF16)] * 4 + [((EMB, FREQ), F32), ((COLS, D), F32)]
    outs = pl.pallas_call(
        kernel,
        out_shape=tuple(pltpu.VMEM(shape, dtype) for shape, dtype in shapes),
        in_specs=[hbm] * 7,
        out_specs=(vmem,) * 6,
        scratch_shapes=[
            pltpu.SMEM((NCLIP,), jnp.int32),
            pltpu.VMEM((EMB, FREQ), BF16),
            pltpu.VMEM((COLS, D), BF16),
            pltpu.VMEM((OWN, 4, CLIP, HEAD), BF16),
            pltpu.VMEM((OWN, 4, CLIP, HEAD), BF16),
            pltpu.VMEM(blocks + (NOWN, HEAD), BF16),
            pltpu.VMEM((NOWN, HEAD), F32),
            pltpu.VMEM((NOWN, D), BF16),
            pltpu.VMEM((NOWN, FREQ), F32),
            pltpu.VMEM((COLS, HEAD), F32),
            pltpu.VMEM((COLS, HEAD), F32),
            pltpu.VMEM(blocks[1:] + (COLS, HEAD), F32),
            pltpu.VMEM((OWN, HEAD, HEAD), F32),
            pltpu.VMEM((8, HEAD), F32),
            pltpu.VMEM((2,) + blocks[1:] + (8, HEAD), F32),
            pltpu.VMEM(blocks + (NOWN, HEAD), F32),
            pltpu.VMEM(blocks[:3] + (NOWN, HEAD), F32),
            pltpu.VMEM(blocks[:2] + (NOWN, HEAD), F32),
            pltpu.VMEM(blocks[:1] + (NOWN, HEAD), F32),
            pltpu.VMEM(blocks[:3] + (NOWN, HEAD), F32),
            pltpu.VMEM((3,) + blocks[:2] + (NOWN, HEAD), F32),
            pltpu.VMEM(blocks[:1] + (NOWN, HEAD), F32),
            pltpu.VMEM((3, NOWN, HEAD), BF16),
            pltpu.VMEM((SPAN, NOWN, HEAD), BF16),
            pltpu.VMEM((NOWN, HEAD), BF16),
            pltpu.VMEM((HEAD, CLIP), BF16),
            pltpu.VMEM((HEAD, CLIP), BF16),
            pltpu.VMEM((CLIP, HEAD), F32),
            pltpu.VMEM((CLIP, HEAD), F32),
            pltpu.SemaphoreType.REGULAR,
            pltpu.SemaphoreType.DMA((4,)),
            pltpu.SemaphoreType.DMA((28,)),
            pltpu.SemaphoreType.DMA((28,)),
            pltpu.SemaphoreType.DMA,
            pltpu.SemaphoreType.DMA((OWN,)),
            pltpu.SemaphoreType.DMA,
            pltpu.SemaphoreType.DMA((4,)),
        ],
        compiler_params=pltpu.CompilerParams(
            collective_id=0, has_side_effects=True, vmem_limit_bytes=40 * 2**20
        ),
    )(
        *[
            pltpu.with_memory_space_constraint(array, pltpu.HBM)
            for array in (
                timestep, query_rows, key_rows, value_rows, cotangent,
                time_weight[0].T, gate_weight[0].T,
            )
        ],
    )
    outs = [pltpu.with_memory_space_constraint(out, pltpu.VMEM) for out in outs]
    outs = pl.pallas_call(
        deliver,
        out_shape=tuple(jax.ShapeDtypeStruct(shape, dtype) for shape, dtype in shapes),
        in_specs=[vmem] * 6,
        out_specs=(hbm,) * 6,
        scratch_shapes=[pltpu.SemaphoreType.DMA((6,))],
        compiler_params=pltpu.CompilerParams(vmem_limit_bytes=4 * 2**20),
    )(*outs)
    gated, query_grad, key_grad, value_grad, time_grad, gate_grad = outs
    return gated, query_grad, key_grad, value_grad, time_grad.T[None], gate_grad.T[None]


def solution(mesh):
    return jax.shard_map(
        per_device,
        mesh=mesh,
        in_specs=(
            P(("expert", "fsdp"), None),
            P(("expert", "fsdp"), None),
            P(("expert", "fsdp"), None),
            P(),
            P("expert", None, "fsdp"),
            P("expert", None, "fsdp"),
            P(("expert", "fsdp"), None),
        ),
        out_specs=(
            P(("expert", "fsdp"), None),
            P(("expert", "fsdp"), None),
            P(("expert", "fsdp"), None),
            P(("expert", "fsdp"), None),
            P("expert", None, "fsdp"),
            P("expert", None, "fsdp"),
        ),
        check_vma=False,
    )
```
